256 devices in a mesh: row: 32 (over z, x), col: 8 (over y, core).
Axes of the slice: x: 4, y: 4, z: 8, core: 2. Of those that a mesh axis runs over, the one named last changes fastest.
Arguments:
- slab: float32 [2, 32, 1024, 2048], P(None, 'row', None, 'col'), may hold values from -6 to 6
- lower_first: bfloat16 [2, 32, 1024, 1024], P(None, 'row', None, 'col'), may hold values from -0.09375 to 0.09375
- lower_second: bfloat16 [2, 32, 1024, 1024], P(None, 'row', None, 'col'), may hold values from -0.09375 to 0.09375
- pivot_rows: int32 [2, 1024], replicated, may hold values from 0 to 65535, as said below
- displaced: int32 [2, 1024], replicated, may hold values from 0 to 65535, as said below
Outputs:
- factored: float32 [2, 32, 1024, 2048], P(None, 'row', None, 'col')
The draws below stay inside these ranges and needn't reach their ends.
Inputs may be any that keep to these rules, and one draw needn't show every extreme that they name: `pivot_rows`: for panel k the 1024 entries are distinct row numbers of at least k * 1024, positions after the interchanges of the earlier panel. At most 48 of them lie on one index of row (row r lies on (r // 1024) % 32), and exactly 48 on some index. `displaced`: completes the interchange of panel k into a permutation: a former pivot block row that is itself a pivot row goes to its pivot position; the others go, one each, to the rows that pivot rows outside the block left.
All inputs are finite; a program needn't handle non-finite values.
Results may differ from the reference program's by a relative error of at most 0.0019.
Values may be sent and summed in bfloat16 or wider, within the bound.
No kernel may reach another device: no remote copies, remote signals or barrier semaphores. Data moves between devices by JAX's collectives and lax.ppermute only.
A program may use at most 128 MiB of HBM per device.

```python
import jax
import jax.numpy as jnp
from jax import lax

NB = 1024
TW = 2048
RCYC = 2
CAP = 48
N_ROW = 32


def pivot_plan(key):
    local_count = RCYC * NB
    pivot_list = []
    moved_list = []
    for number in range(2):
        panel_key = jax.random.fold_in(key, 100 + number)
        key_busy, key_pool, key_order, key_rows, key_first = jax.random.split(panel_key, 5)
        busiest = jax.random.randint(key_busy, (), 0, N_ROW).astype(jnp.int32)
        others = jnp.arange(N_ROW - 1, dtype=jnp.int32)
        others = others + (others >= busiest).astype(jnp.int32)
        slot_pool = jnp.repeat(others, CAP)
        chosen = jax.random.permutation(key_pool, slot_pool)[:NB - CAP]
        labels = jnp.concatenate([jnp.full((CAP,), busiest, jnp.int32), chosen])
        labels = jax.random.permutation(key_order, labels).astype(jnp.int32)
        one_hot = (labels[:, None] == jnp.arange(N_ROW, dtype=jnp.int32)[None, :]).astype(jnp.int32)
        ordinal = jnp.sum((jnp.cumsum(one_hot, axis=0) - 1) * one_hot, axis=1)
        shuffles = jax.vmap(lambda k: jax.random.permutation(k, local_count))(jax.random.split(key_rows, N_ROW))
        local_rows = shuffles[labels, ordinal].astype(jnp.int32)
        if number == 1:
            spared = (NB + jax.random.permutation(key_first, local_count - NB)).astype(jnp.int32)
            local_rows = jnp.where(labels == 0, spared[ordinal], local_rows)
        pivots = (local_rows // NB * N_ROW + labels) * NB + local_rows % NB
        first_row = number * NB
        top_slots = jnp.arange(NB, dtype=jnp.int32)
        in_top = (pivots >= first_row) & (pivots < first_row + NB)
        goes_to = jnp.full((NB,), -1, jnp.int32).at[jnp.where(in_top, pivots - first_row, NB)].set(first_row + top_slots, mode='drop')
        free_top = goes_to < 0
        free_rank = jnp.cumsum(free_top.astype(jnp.int32)) - 1
        outside = jnp.logical_not(in_top)
        out_rank = jnp.cumsum(outside.astype(jnp.int32)) - 1
        outside_rows = jnp.zeros((NB,), jnp.int32).at[jnp.where(outside, out_rank, NB)].set(pivots, mode='drop')
        moved_to = jnp.where(free_top, outside_rows[jnp.maximum(free_rank, 0)], goes_to)
        pivot_list.append(pivots)
        moved_list.append(moved_to)
    return (jnp.stack(pivot_list), jnp.stack(moved_list))


def draw_pivot_rows(key, part):
    shared = pivot_plan(key)
    return shared[0]


def draw_displaced(key, part):
    shared = pivot_plan(key)
    return shared[1]


def levels(stream_key, dims, shards, smallest, high):
    gain, own = 1.0, jax.random.fold_in(stream_key, 6)
    for position, blocks in shards:
        steps = jnp.exp(jax.random.uniform(jax.random.fold_in(own, position), (blocks,), jnp.float32, smallest / len(shards), high / len(shards)))
        gain = gain * jnp.repeat(steps, dims[position] // blocks).reshape([-1 if axis == position else 1 for axis in range(len(dims))])
    return gain


def scatter_about(own_key, shape, deviation, limit, shards=(), held_as=jnp.bfloat16):
    values = jax.random.normal(own_key, shape, jnp.float32) * deviation
    if len(shards) > 0:
        values = levels(own_key, shape, shards, -0.22, 0.18) * values
    return jnp.clip(values, min=-limit, max=limit).astype(held_as)


def setup_inputs(seed: int = 0) -> dict:
    splits = jax.random.split(jax.random.key(seed), 6)
    slab = scatter_about(splits[0], (RCYC, N_ROW, NB, TW), 1.0, 6.0, ((1, 32), (3, 8)), jnp.float32)
    lower_first = scatter_about(splits[1], (RCYC, N_ROW, NB, NB), (4 * NB) ** -0.5, 0.09375, ((1, 32), (3, 8)))
    lower_second = scatter_about(splits[2], (RCYC, N_ROW, NB, NB), (4 * NB) ** -0.5, 0.09375, ((1, 32), (3, 8)))
    pivot_rows = draw_pivot_rows(jax.random.fold_in(splits[5], 71), 0)
    displaced = draw_displaced(jax.random.fold_in(splits[5], 71), 0)
    return dict(slab=slab, lower_first=lower_first, lower_second=lower_second, pivot_rows=pivot_rows, displaced=displaced)


def unit_lower_solve(lower_part, right_part):
    extent = lower_part.shape[0]
    tile_size = min(128, extent)
    tile_count = extent // tile_size
    strict = jnp.tril(lower_part, -1)
    nilpotent = -jnp.stack([strict[i * tile_size:(i + 1) * tile_size, i * tile_size:(i + 1) * tile_size] for i in range(tile_count)])
    identity = jnp.eye(tile_size, dtype=lower_part.dtype)
    inverses = identity + nilpotent
    powered = nilpotent
    for j in range(tile_size.bit_length() - 2):
        powered = jnp.einsum("bij,bjk->bik", powered, powered, precision=lax.Precision.HIGHEST)
        inverses = jnp.einsum("bij,bjk->bik", inverses, identity + powered, precision=lax.Precision.HIGHEST)
    pieces = []
    for i in range(tile_count):
        residue = right_part[i * tile_size:(i + 1) * tile_size]
        if i > 0:
            earlier = jnp.concatenate(pieces, axis=0)
            residue = residue - jnp.dot(strict[i * tile_size:(i + 1) * tile_size, :i * tile_size], earlier, precision=lax.Precision.HIGHEST)
        pieces.append(jnp.dot(inverses[i], residue, precision=lax.Precision.HIGHEST))
    return jnp.concatenate(pieces, axis=0)


def reference(slab, lower_first, lower_second, pivot_rows, displaced):
    total_rows = RCYC * N_ROW * NB
    tile_cols = min(512, TW)
    tiles = slab.reshape(total_rows, TW // tile_cols, tile_cols).transpose(1, 0, 2)
    top_slots = jnp.arange(NB, dtype=jnp.int32)
    identity_order = jnp.arange(total_rows, dtype=jnp.int32)
    panels = (lower_first.reshape(total_rows, NB), lower_second.reshape(total_rows, NB))
    sources = []
    for number in range(2):
        first_row = number * NB
        order_now = identity_order.at[first_row + top_slots].set(pivot_rows[number].astype(jnp.int32))
        sources.append(order_now.at[displaced[number].astype(jnp.int32)].set(first_row + top_slots))

    def factor_tile(matrix):
        for number in range(2):
            first_row = number * NB
            matrix = matrix[sources[number]]
            diag_lower = panels[number][first_row:first_row + NB].astype(jnp.float32)
            solved = unit_lower_solve(diag_lower, matrix[first_row:first_row + NB])
            solved_low = solved.astype(jnp.bfloat16)
            beneath = matrix[first_row + NB:] - jnp.dot(panels[number][first_row + NB:], solved_low, preferred_element_type=jnp.float32)
            matrix = jnp.concatenate([matrix[:first_row], solved, beneath], axis=0)
        return matrix

    result = lax.map(factor_tile, tiles)
    return result.transpose(1, 0, 2).reshape(RCYC, N_ROW, NB, TW)
```

```python
import functools

import jax
import jax.numpy as jnp
from jax import lax
from jax.experimental import pallas as pl
from jax.experimental.pallas import tpu as pltpu
from jax.sharding import PartitionSpec as P

NB = 1024
CAP = 48
NX, NZ, NY = 4, 8, 4
TILE = 128
LANES = 128
CHUNK = 512
FLOCK = NX * CAP
HALF = NB // 2
GROUP = NZ * CAP
COLS = 256
PART = COLS // NX
BF16, F32, I32 = jnp.bfloat16, jnp.float32, jnp.int32


def at(z, x):
    return (z % NZ) * NX + x % NX


def mm(a, b):
    return jnp.dot(a, b, preferred_element_type=F32)


def mm_t(a, b):
    return lax.dot_general(a, b, (((0,), (0,)), ((), ())), preferred_element_type=F32)


def iota(shape, axis):
    return lax.broadcasted_iota(I32, shape, axis)


def hot(mask):
    return jnp.where(mask, 1.0, 0.0).astype(BF16)


def split(value):
    high = value.astype(BF16)
    return high, (value - high.astype(F32)).astype(BF16)


def call(kernel, outs, *args, name, scratch=(), mib=20, **blocks):
    size = lambda a: a.size * a.dtype.itemsize
    return pl.pallas_call(
        kernel,
        out_shape=[jax.ShapeDtypeStruct(s, d) for s, d in outs],
        scratch_shapes=list(scratch),
        compiler_params=pltpu.CompilerParams(vmem_limit_bytes=mib * 2**20),
        cost_estimate=pl.CostEstimate(
            flops=0, bytes_accessed=sum(size(a) for a in args), transcendentals=0
        ),
        name=name,
        **blocks,
    )(*args)


def place_in(rows):
    return ((rows >> 15) << 10) | (rows & (NB - 1))


def owner_of(rows):
    return (rows >> 10) & 31


def x_major(owner, rank):
    return ((owner & (NX - 1)) * NZ + (owner >> 2)) * CAP + rank


def index_kernel(rows_ref, slot_ref, order_ref, from_ref, to_ref):
    me = lax.axis_index("row")
    cols = rows_ref[...].astype(F32).T.astype(I32)
    lane = iota((NB, LANES), 1)
    owners = jnp.zeros((NB, LANES), I32)
    for k in range(4):
        owners = jnp.where(lane >> 5 == k, owner_of(cols[:, k : k + 1]), owners)
    own = jnp.where(owners == (lane & 31), 1.0, 0.0)
    earlier = hot(iota((TILE, TILE), 1) < iota((TILE, TILE), 0))
    before, count = [], jnp.zeros((1, LANES), F32)
    for i in range(NB // TILE):
        part = own[i * TILE : (i + 1) * TILE]
        before.append((mm(earlier, part.astype(BF16)) + count) * part)
        count = count + jnp.sum(part, axis=0, keepdims=True)
    before = jnp.concatenate(before, axis=0)
    slots, lists = jnp.zeros((NB, LANES), I32), jnp.zeros((LANES, LANES), I32)
    row, line = iota((8, NB), 0), iota((LANES, LANES), 0)
    for k in range(4):
        owner = owner_of(cols[:, k : k + 1])
        rank = jnp.sum(jnp.where(lane >> 5 == k, before, 0.0), axis=1, keepdims=True).astype(I32)
        slots = jnp.where(lane == k, x_major(owner, rank), slots)
        mine = hot((owner == me) & (rank == lane) & (lane < CAP))
        place = place_in(rows_ref[k : k + 1, :])
        parts = jnp.where(row == 0, place >> 6, jnp.where(row == 1, place & 63, 1))
        found = mm(parts.astype(F32).astype(BF16), mine).astype(I32)
        places = jnp.where(found[2:3] > 0, found[:1] * 64 + found[1:2], -1)
        lists = jnp.where(line == k, places, lists)
    slot_ref[...] = slots
    order_ref[...] = slots.astype(F32).T[:8].astype(I32)
    to_ref[...] = lists[:8]
    from_ref[...] = lists.astype(F32).T.astype(I32)


def pick(number, from_ref, start, rows):
    select = hot(from_ref[:, 2 * number : 2 * number + 1] == iota((LANES, rows.shape[0]), 1) + start)
    high, low = split(rows)
    return mm(select, high), mm(select, low)


def pick_kernel(matrix_ref, from_ref, picked_ref):
    def step(i, totals):
        start = pl.multiple_of(i * CHUNK, CHUNK)
        high, low = pick(0, from_ref, start, matrix_ref[pl.ds(start, CHUNK), :])
        return totals[0] + high, totals[1] + low

    none = jnp.zeros((LANES, COLS), F32)
    high, low = lax.fori_loop(0, 2 * NB // CHUNK, step, (none, none))
    picked_ref[:CAP] = high[:CAP].astype(BF16)
    picked_ref[CAP:] = low[:CAP].astype(BF16)


def down(number, z, top, order_ref):
    line = iota((FLOCK, 1), 0)
    slot = line + z * CAP
    for k in range(1, NX):
        slot = slot + jnp.where(line >= k * CAP, GROUP - CAP, 0)
    order = order_ref[2 * number + 1 : 2 * number + 2, :]
    return mm(hot(order == slot), top).astype(BF16)


def first_front_kernel(top_ref, order_ref, b0, b1, b2, b3, joined_ref, own_ref, *outs):
    for x, ref in enumerate((b0, b1, b2, b3)):
        joined_ref[x * CAP : (x + 1) * CAP, :COLS] = ref[:CAP]
        joined_ref[x * CAP : (x + 1) * CAP, COLS:] = ref[CAP:]
    own_ref[...] = jnp.zeros_like(own_ref)
    is_root = lax.axis_index("row") == 0

    @pl.when(is_root)
    def _():
        top = top_ref[...].astype(BF16)
        own_ref[...] = down(0, 0, top, order_ref)
        for z, ref in enumerate(outs):
            ref[:, :COLS] = down(0, z + 1, top, order_ref)
            ref[:, COLS:] = jnp.zeros((FLOCK, COLS), BF16)

    @pl.when(jnp.logical_not(is_root))
    def _():
        for ref in outs:
            ref[...] = joined_ref[...]


def last_down_kernel(top_ref, order_ref, out_ref):
    out_ref[...] = jnp.zeros_like(out_ref)

    @pl.when(lax.axis_index("row") == 1)
    def _():
        top = top_ref[...].astype(BF16)
        for z in range(NZ):
            rows = down(1, z, top, order_ref)
            out_ref[2 * z * FLOCK : (2 * z + 1) * FLOCK] = rows[:, :LANES]
            out_ref[(2 * z + 1) * FLOCK : (2 * z + 2) * FLOCK] = rows[:, LANES:]


def cut_kernel(*refs):
    picked, outs = refs[:NZ], refs[NZ:]
    x = lax.axis_index("row") & (NX - 1)
    high = jnp.concatenate([p[:CAP] for p in picked], axis=0)
    low = jnp.concatenate([p[CAP:] for p in picked], axis=0)
    row, lane = iota((COLS, LANES), 0), iota((COLS, LANES), 1)
    for s, ref in enumerate(outs):
        first = ((x + s) & (NX - 1)) * PART
        left = hot((row == first + lane) & (lane < PART))
        right = hot((row == first + lane - PART) & (lane >= PART))
        ref[...] = (mm(high, left) + mm(low, right)).astype(BF16)


def mm3(a, b):
    a_high, a_low = split(a)
    b_high, b_low = split(b)
    return mm(a_high, b_high) + (mm(a_high, b_low) + mm(a_low, b_high))


def inverse_kernel(diag_ref, high_ref, low_ref):
    row, lane = iota((TILE, TILE), 0), iota((TILE, TILE), 1)
    identity = jnp.where(lane == row, 1.0, 0.0)
    powers = []
    for i in range(NB // TILE):
        part = slice(i * TILE, (i + 1) * TILE)
        powers.append(jnp.where(lane < row, -diag_ref[part, part].astype(F32), 0.0))
    inverses = [identity + p for p in powers]
    for _ in range(TILE.bit_length() - 2):
        powers = [mm3(p, p) for p in powers]
        inverses = [v + mm3(v, p) for v, p in zip(inverses, powers)]
    size = TILE
    while size < NB:
        none = jnp.zeros((size, size), F32)
        joined = []
        for i in range(0, len(inverses), 2):
            upper, lower = inverses[i], inverses[i + 1]
            between = diag_ref[(i + 1) * size : (i + 2) * size, i * size : (i + 1) * size]
            high, low = split(upper)
            corner = mm3(lower, mm(between, high) + mm(between, low))
            joined.append(
                jnp.concatenate(
                    [
                        jnp.concatenate([upper, none], axis=1),
                        jnp.concatenate([-corner, lower], axis=1),
                    ],
                    axis=0,
                )
            )
        inverses, size = joined, 2 * size
    high_ref[...], low_ref[...] = split(inverses[0])


def first_solve_kernel(high_ref, low_ref, slot_ref, *refs):
    parts, outs, (gathered_ref, right_ref, select_ref) = refs[:NZ], refs[NZ : NZ + NX], refs[NZ + NX :]
    lane = iota((1, FLOCK), 1)
    for k in range(1, NX):
        lane = lane + jnp.where(iota((1, FLOCK), 1) >= k * CAP, GROUP - CAP, 0)
    for z, ref in enumerate(parts):
        gathered_ref[z * FLOCK : (z + 1) * FLOCK] = ref[...]
        select_ref[:, z * FLOCK : (z + 1) * FLOCK] = hot(slot_ref[:, :1] == lane + z * CAP)
    for i in range(0, NB, HALF):
        found = mm(select_ref[i : i + HALF], gathered_ref[...])
        high, low = split(found[:, :COLS] + found[:, COLS:])
        right_ref[i : i + HALF, :COLS] = high
        right_ref[i : i + HALF, COLS:] = low
    halves = []
    for i in range(0, NB, HALF):
        wide = mm(high_ref[i : i + HALF], right_ref[...])
        halves.append(wide[:, :COLS] + (wide[:, COLS:] + mm(low_ref[i : i + HALF], right_ref[:, :COLS])))
    left = iota((HALF, LANES), 1) < PART
    for x, ref in enumerate(outs):
        block = slice(x // 2 * LANES, (x // 2 + 1) * LANES)
        upper, lower = halves[0][:, block], halves[1][:, block]
        if x % 2 == 0:
            ref[...] = jnp.where(left, upper, pltpu.roll(lower, PART, 1)).astype(BF16)
        else:
            ref[...] = jnp.where(left, pltpu.roll(upper, PART, 1), lower).astype(BF16)


def both(value):
    return value + pltpu.roll(value, PART, 1)


def last_solve_kernel(high_ref, low_ref, slot_ref, down_ref, c0, c1, c2, c3, *refs):
    outs, (gathered_ref, select_ref) = refs[:NZ], refs[NZ:]
    x = lax.axis_index("row") & (NX - 1)
    for s, ref in enumerate((c0, c1, c2, c3)):
        part = slice(s * GROUP, (s + 1) * GROUP)
        first = ((x - s) & (NX - 1)) * GROUP
        gathered_ref[part] = ref[...]
        select_ref[:, part] = hot(slot_ref[:, 2:3] == iota((1, GROUP), 1) + first)
    high, low = split(both(mm(select_ref[...], gathered_ref[...])))
    parts = jnp.where(iota((NB, LANES), 1) < PART, high, low)
    solved = both(mm(high_ref[...], parts)) + mm(low_ref[...], high)
    left = iota((HALF, LANES), 1) < PART
    solved = jnp.where(left, solved[:HALF], solved[HALF:]).astype(BF16)
    for z, ref in enumerate(outs):
        ref[:HALF] = solved
        ref[HALF:] = down_ref[2 * z * FLOCK : 2 * (z + 1) * FLOCK]


def pass_on(solved, rows_ref, outs):
    x = lax.axis_index("row") & (NX - 1)
    for s, ref in enumerate(outs):
        start = pl.multiple_of(((x + s) & (NX - 1)) * CAP, CAP)
        rows = rows_ref[pl.ds(start, CAP), :]
        ref[:HALF] = solved
        ref[HALF : HALF + CAP] = rows[:, :LANES]
        ref[HALF + CAP :] = rows[:, LANES:]


def sum_of(refs, part):
    total = refs[0][part]
    for ref in refs[1:]:
        total = total + ref[part]
    return total


def first_relay_kernel(own_ref, down_ref, *refs):
    came, downs, outs, rows_ref = refs[: NZ - 1], refs[NZ - 1 : 2 * NZ - 2], refs[2 * NZ - 2 : -1], refs[-1]
    me = lax.axis_index("row")
    every = slice(None)
    rows_ref[...] = jnp.where(me == 0, down_ref[...], sum_of(downs, (every, slice(COLS))))
    pass_on(jnp.where(me < NX, own_ref[...], sum_of(came, every)), rows_ref, outs)


def last_relay_kernel(own_ref, *refs):
    came, outs, rows_ref = refs[: NZ - 1], refs[NZ - 1 : -1], refs[-1]
    front = lax.axis_index("row") < NX
    message = jnp.where(front, own_ref[...], sum_of(came, slice(None)))
    rows_ref[:, :LANES] = message[HALF : HALF + FLOCK]
    rows_ref[:, LANES:] = message[HALF + FLOCK :]
    pass_on(message[:HALF], rows_ref, outs)


def receive(pieces, u_ref, down_ref):
    x = lax.axis_index("row") & (NX - 1)
    row, lane = iota((LANES, COLS), 0), iota((LANES, COLS), 1)
    above, below = jnp.zeros((HALF, COLS), F32), jnp.zeros((HALF, COLS), F32)
    for s, ref in enumerate(pieces):
        first = ((x - s) & (NX - 1)) * PART
        piece = ref[:HALF]
        above = above + mm(piece, hot((lane == first + row) & (row < PART)))
        below = below + mm(piece, hot((lane == first + row - PART) & (row >= PART)))
    u_ref[:HALF] = above.astype(BF16)
    u_ref[HALF:] = below.astype(BF16)
    down_ref[:CAP, :LANES] = sum_of(pieces, slice(HALF, HALF + CAP))
    down_ref[:CAP, LANES:] = sum_of(pieces, slice(HALF + CAP, HALF + 2 * CAP))
    down_ref[CAP:] = jnp.zeros((LANES - CAP, COLS), BF16)


def update(number, matrix_ref, to_ref, pieces, lower_refs, out_ref, scratch, then):
    u_ref, down_ref, rows_ref, lower_ref, rows_sem, lower_sem, out_sem = scratch
    me = lax.axis_index("row")
    count = 2 * NB // CHUNK
    each = count // len(lower_refs)

    def rows_of(i):
        return pl.ds(pl.multiple_of(i * CHUNK, CHUNK), CHUNK)

    def rows_copy(i):
        return pltpu.make_async_copy(matrix_ref.at[rows_of(i)], rows_ref.at[rows_of(i)], rows_sem.at[i])

    def out_copy(i):
        return pltpu.make_async_copy(rows_ref.at[rows_of(i)], out_ref.at[rows_of(i)], out_sem.at[i])

    for i in range(count):
        rows_copy(i).start()
        source = lower_refs[i // each].at[rows_of(i % each)]
        pltpu.make_async_copy(source, lower_ref.at[rows_of(i)], lower_sem.at[i]).start()
    receive(pieces, u_ref, down_ref)

    def step(i, carry):
        here = to_ref[2 * number + 1 : 2 * number + 2, :] == iota((CHUNK, LANES), 0) + i * CHUNK
        there = jnp.max(jnp.where(here, 1.0, 0.0), axis=1, keepdims=True) > 0.5
        moved = mm(hot(here), down_ref[...])
        rows_copy(i).wait()
        pltpu.make_async_copy(lower_ref.at[rows_of(i)], lower_ref.at[rows_of(i)], lower_sem.at[i]).wait()
        old = rows_ref[rows_of(i), :]
        new = jnp.where(there, moved, old) - mm(lower_ref[rows_of(i), :], u_ref[...])
        in_top = i < NB // CHUNK
        top = u_ref[rows_of(i & (NB // CHUNK - 1)), :].astype(F32)
        new = jnp.where(in_top & (me == number), top, jnp.where(in_top & (me < number), old, new))
        rows_ref[rows_of(i), :] = new
        out_copy(i).start()
        return then(i, new, carry)

    none = jnp.zeros((LANES, COLS), F32)
    carry = lax.fori_loop(0, count, step, (none, none), unroll=True)
    for i in range(count):
        out_copy(i).wait()
    return carry


def first_update_kernel(
    matrix_ref, to_ref, from_ref, m0, m1, m2, m3, top_ref, low_ref, out_ref, picked_ref, *scratch
):
    def then(i, rows, carry):
        high, low = pick(1, from_ref, i * CHUNK, rows)
        return carry[0] + high, carry[1] + low

    lowers = (top_ref, low_ref)
    high, low = update(0, matrix_ref, to_ref, (m0, m1, m2, m3), lowers, out_ref, scratch, then)
    picked_ref[:CAP] = high[:CAP].astype(BF16)
    picked_ref[CAP:] = low[:CAP].astype(BF16)


def last_update_kernel(matrix_ref, to_ref, m0, m1, m2, m3, lower_ref, out_ref, *scratch):
    then = lambda i, rows, carry: carry
    update(1, matrix_ref, to_ref, (m0, m1, m2, m3), (lower_ref,), out_ref, scratch, then)


def send(value, pairs):
    return lax.ppermute(value, "row", pairs)


def over_x(root_x, pieces):
    return [pieces[root_x]] + [
        send(pieces[(root_x + s) % NX], [(at(0, root_x), at(0, root_x + s))]) for s in range(1, NX)
    ]


def in_hbm(a):
    return pltpu.with_memory_space_constraint(a, pltpu.HBM)


def from_front(messages):
    return [messages[0]] + [
        send(messages[z], [(at(0, x), at(z, x)) for x in range(NX)]) for z in range(1, NZ)
    ]


def along_x(messages):
    return [messages[0]] + [
        send(messages[s], [(at(z, x), at(z, x + s)) for z in range(NZ) for x in range(NX)])
        for s in range(1, NX)
    ]


def local(slab, lower_first, lower_second, pivot_rows, displaced):
    row = lax.axis_index("row")
    matrix = slab.reshape(2 * NB, COLS)
    first, second = [p.reshape(2 * NB, p.shape[3]) for p in (lower_first, lower_second)]
    gather = lambda block: lax.all_gather(block, "col", axis=1, tiled=True)
    inverse = lambda d: call(inverse_kernel, [((NB, NB), BF16)] * 2, d, name="inverse", mib=32)
    picked_shape = ((2 * CAP, COLS), BF16)
    there, vmem = pl.BlockSpec(memory_space=pl.ANY), pl.BlockSpec(memory_space=pltpu.VMEM)
    block_of_top = pl.BlockSpec((NB, COLS), lambda i: (0, 0))
    update_scratch = [
        pltpu.VMEM((NB, COLS), BF16),
        pltpu.VMEM((LANES, COLS), BF16),
        pltpu.VMEM((2 * NB, COLS), F32),
        pltpu.VMEM((2 * NB, NB), BF16),
    ] + [pltpu.SemaphoreType.DMA((2 * NB // CHUNK,))] * 3
    relayed = [((HALF + 2 * CAP, LANES), BF16)] * NX
    relay_scratch = [pltpu.VMEM((FLOCK, COLS), BF16)]

    blocks = over_x(1, [second[:NB]] * NX)
    rows = jnp.stack([pivot_rows, displaced], axis=1).reshape(4, NB)
    rows = jnp.concatenate([rows, rows], axis=0)
    slot, order, pivots, targets = call(
        index_kernel,
        [((NB, LANES), I32), ((8, NB), I32), ((LANES, LANES), I32), ((8, LANES), I32)],
        rows,
        name="index",
    )
    (picked,) = call(pick_kernel, [picked_shape], matrix, pivots, name="pick")
    blocks, picked = lax.optimization_barrier((blocks, picked))
    top, low = gather(first[:NB]), gather(first[NB:])

    by_x = [picked] + [
        send(picked, [(at(z, x + s), at(z, x)) for z in range(NZ) for x in range(NX)]) for s in range(1, NX)
    ]
    joined, own_down, *messages = call(
        first_front_kernel,
        [((FLOCK, 2 * COLS), BF16), ((FLOCK, COLS), BF16)] + [((FLOCK, 2 * COLS), BF16)] * (NZ - 1),
        matrix,
        order,
        *by_x,
        name="front",
        in_specs=[block_of_top] + [vmem] * 5,
        grid=(1,),
    )
    parts = [
        send(message, [(at(z, 0), at(0, 0)), (at(0, 0), at(z, 0))]) for z, message in enumerate(messages, 1)
    ]
    inverses, parts = lax.optimization_barrier((inverse(top), parts))
    solved = call(
        first_solve_kernel,
        [((HALF, LANES), BF16)] * NX,
        *inverses,
        slot,
        joined,
        *parts,
        name="solve",
        scratch=[pltpu.VMEM((NX * GROUP, 2 * COLS), BF16), pltpu.VMEM((NB, 2 * COLS), BF16)]
        + [pltpu.VMEM((NB, NX * GROUP), BF16)],
        mib=32,
    )
    pieces = over_x(0, solved)
    piece = pieces[0]
    for s in range(1, NX):
        piece = jnp.where(row == s, pieces[s], piece)
    came = from_front([piece] * NZ)
    messages = call(
        first_relay_kernel, relayed, piece, own_down, *came[1:], *parts, name="relay", scratch=relay_scratch
    )
    block = blocks[0]
    for s in range(1, NX):
        block = jnp.where(row == (1 + s) % NX, blocks[s], block)
    block, late = lax.optimization_barrier((block, second))
    diag, lower = gather(block), in_hbm(gather(late))
    top, low = in_hbm(top), in_hbm(low)
    matrix, picked = call(
        first_update_kernel,
        [((2 * NB, COLS), F32), picked_shape],
        matrix,
        targets,
        pivots,
        *along_x(messages),
        top,
        low,
        name="update",
        scratch=update_scratch,
        in_specs=[there] + [vmem] * 6 + [there] * 2,
        out_specs=[there, vmem],
    )

    came = [picked] + [
        send(picked, [(at(z, x), at(0, x)) for x in range(NX)]) for z in range(1, NZ)
    ]
    (downs,) = call(
        last_down_kernel,
        [((2 * NZ * FLOCK, LANES), BF16)],
        matrix,
        order,
        name="down",
        in_specs=[block_of_top, vmem],
        grid=(1,),
    )
    diag, downs = lax.optimization_barrier((diag, downs))
    inverses, came = lax.optimization_barrier((inverse(diag), came))
    cuts = call(cut_kernel, [((GROUP, LANES), BF16)] * NX, *came, name="cut")
    cuts = [cuts[0]] + [
        send(cuts[s], [(at(0, x), at(0, x + s)) for x in range(NX)]) for s in range(1, NX)
    ]
    messages = call(
        last_solve_kernel,
        [((HALF + 2 * FLOCK, LANES), BF16)] * NZ,
        *inverses,
        slot,
        downs,
        *cuts,
        name="solve",
        scratch=[pltpu.VMEM((NX * GROUP, LANES), BF16), pltpu.VMEM((NB, NX * GROUP), BF16)],
    )
    messages = call(last_relay_kernel, relayed, *from_front(messages), name="relay", scratch=relay_scratch)
    (matrix,) = call(
        last_update_kernel,
        [((2 * NB, COLS), F32)],
        matrix,
        targets,
        *along_x(messages),
        lower,
        name="update",
        scratch=update_scratch,
        in_specs=[there] + [vmem] * 5 + [there],
        out_specs=[there],
    )
    return matrix.reshape(2, 1, NB, COLS)


def solution(mesh):
    placed = (
        P(None, "row", None, "col"),
        P(None, "row", None, "col"),
        P(None, "row", None, "col"),
        P(),
        P(),
    )
    return jax.shard_map(
        local, mesh=mesh, in_specs=placed, out_specs=P(None, "row", None, "col"), check_vma=False
    )
```

```python
import functools

import jax
import jax.numpy as jnp
from jax import lax
from jax.experimental import pallas as pl
from jax.experimental.pallas import tpu as pltpu
from jax.sharding import PartitionSpec as P

NB = 1024
CAP = 48
NX, NZ, NY = 4, 8, 4
TILE = 128
LANES = 128
CHUNK = 512
FLOCK = NX * CAP
HALF = NB // 2
GROUP = NZ * CAP
COLS = 256
PART = COLS // NX
BF16, F32, I32 = jnp.bfloat16, jnp.float32, jnp.int32


def at(z, x):
    return (z % NZ) * NX + x % NX


def mm(a, b):
    return jnp.dot(a, b, preferred_element_type=F32)


def mm_t(a, b):
    return lax.dot_general(a, b, (((0,), (0,)), ((), ())), preferred_element_type=F32)


def iota(shape, axis):
    return lax.broadcasted_iota(I32, shape, axis)


def hot(mask):
    return jnp.where(mask, 1.0, 0.0).astype(BF16)


def split(value):
    high = value.astype(BF16)
    return high, (value - high.astype(F32)).astype(BF16)


def call(kernel, outs, *args, name, scratch=(), mib=10, **blocks):
    size = lambda a: a.size * a.dtype.itemsize
    return pl.pallas_call(
        kernel,
        out_shape=[jax.ShapeDtypeStruct(s, d) for s, d in outs],
        scratch_shapes=list(scratch),
        compiler_params=pltpu.CompilerParams(vmem_limit_bytes=mib * 2**20),
        cost_estimate=pl.CostEstimate(
            flops=0, bytes_accessed=sum(size(a) for a in args), transcendentals=0
        ),
        name=name,
        **blocks,
    )(*args)


def place_in(rows):
    return ((rows >> 15) << 10) | (rows & (NB - 1))


def owner_of(rows):
    return (rows >> 10) & 31


def x_major(owner, rank):
    return ((owner & (NX - 1)) * NZ + (owner >> 2)) * CAP + rank


def index_kernel(rows_ref, slot_ref, order_ref, from_ref, to_ref):
    me = lax.axis_index("row")
    cols = rows_ref[...].astype(F32).T.astype(I32)
    lane = iota((NB, LANES), 1)
    owners = jnp.zeros((NB, LANES), I32)
    for k in range(4):
        owners = jnp.where(lane >> 5 == k, owner_of(cols[:, k : k + 1]), owners)
    own = jnp.where(owners == (lane & 31), 1.0, 0.0)
    earlier = hot(iota((TILE, TILE), 1) < iota((TILE, TILE), 0))
    before, count = [], jnp.zeros((1, LANES), F32)
    for i in range(NB // TILE):
        part = own[i * TILE : (i + 1) * TILE]
        before.append((mm(earlier, part.astype(BF16)) + count) * part)
        count = count + jnp.sum(part, axis=0, keepdims=True)
    before = jnp.concatenate(before, axis=0)
    slots, lists = jnp.zeros((NB, LANES), I32), jnp.zeros((LANES, LANES), I32)
    row, line = iota((8, NB), 0), iota((LANES, LANES), 0)
    for k in range(4):
        owner = owner_of(cols[:, k : k + 1])
        rank = jnp.sum(jnp.where(lane >> 5 == k, before, 0.0), axis=1, keepdims=True).astype(I32)
        slots = jnp.where(lane == k, x_major(owner, rank), slots)
        mine = hot((owner == me) & (rank == lane) & (lane < CAP))
        place = place_in(rows_ref[k : k + 1, :])
        parts = jnp.where(row == 0, place >> 6, jnp.where(row == 1, place & 63, 1))
        found = mm(parts.astype(F32).astype(BF16), mine).astype(I32)
        places = jnp.where(found[2:3] > 0, found[:1] * 64 + found[1:2], -1)
        lists = jnp.where(line == k, places, lists)
    slot_ref[...] = slots
    order_ref[...] = slots.astype(F32).T[:8].astype(I32)
    to_ref[...] = lists[:8]
    from_ref[...] = lists.astype(F32).T.astype(I32)


def pick(number, from_ref, start, rows):
    select = hot(from_ref[:, 2 * number : 2 * number + 1] == iota((LANES, rows.shape[0]), 1) + start)
    high, low = split(rows)
    return mm(select, high), mm(select, low)


def pick_kernel(matrix_ref, from_ref, picked_ref):
    def step(i, totals):
        start = pl.multiple_of(i * CHUNK, CHUNK)
        high, low = pick(0, from_ref, start, matrix_ref[pl.ds(start, CHUNK), :])
        return totals[0] + high, totals[1] + low

    none = jnp.zeros((LANES, COLS), F32)
    high, low = lax.fori_loop(0, 2 * NB // CHUNK, step, (none, none))
    picked_ref[:CAP] = high[:CAP].astype(BF16)
    picked_ref[CAP:] = low[:CAP].astype(BF16)


def down(number, z, top, order_ref):
    line = iota((FLOCK, 1), 0)
    slot = line + z * CAP
    for k in range(1, NX):
        slot = slot + jnp.where(line >= k * CAP, GROUP - CAP, 0)
    order = order_ref[2 * number + 1 : 2 * number + 2, :]
    return mm(hot(order == slot), top).astype(BF16)


def first_front_kernel(top_ref, order_ref, b0, b1, b2, b3, joined_ref, own_ref, *outs):
    for s, ref in enumerate((b0, b1, b2, b3)):
        joined_ref[s * CAP : (s + 1) * CAP, :COLS] = ref[:CAP]
        joined_ref[s * CAP : (s + 1) * CAP, COLS:] = ref[CAP:]
    own_ref[...] = jnp.zeros_like(own_ref)
    is_root = lax.axis_index("row") == 0

    @pl.when(is_root)
    def _():
        top = top_ref[...].astype(BF16)
        own_ref[...] = down(0, 0, top, order_ref)
        for z, ref in enumerate(outs):
            ref[:, :COLS] = down(0, z + 1, top, order_ref)
            ref[:, COLS:] = jnp.zeros((FLOCK, COLS), BF16)

    @pl.when(jnp.logical_not(is_root))
    def _():
        for ref in outs:
            ref[...] = joined_ref[...]


def last_down_kernel(top_ref, order_ref, out_ref):
    out_ref[...] = jnp.zeros_like(out_ref)

    @pl.when(lax.axis_index("row") == 1)
    def _():
        top = top_ref[...].astype(BF16)
        for z in range(NZ):
            rows = down(1, z, top, order_ref)
            out_ref[2 * z * FLOCK : (2 * z + 1) * FLOCK] = rows[:, :LANES]
            out_ref[(2 * z + 1) * FLOCK : (2 * z + 2) * FLOCK] = rows[:, LANES:]


def cut_kernel(*refs):
    picked, outs = refs[:NZ], refs[NZ:]
    x = lax.axis_index("row") & (NX - 1)
    high = jnp.concatenate([p[:CAP] for p in picked], axis=0)
    low = jnp.concatenate([p[CAP:] for p in picked], axis=0)
    row, lane = iota((COLS, LANES), 0), iota((COLS, LANES), 1)
    for s, ref in enumerate(outs):
        first = ((x + s) & (NX - 1)) * PART
        left = hot((row == first + lane) & (lane < PART))
        right = hot((row == first + lane - PART) & (lane >= PART))
        ref[...] = (mm(high, left) + mm(low, right)).astype(BF16)


def mm3(a, b):
    a_high, a_low = split(a)
    b_high, b_low = split(b)
    return mm(a_high, b_high) + (mm(a_high, b_low) + mm(a_low, b_high))


def inverse_kernel(diag_ref, high_ref, low_ref):
    row, lane = iota((TILE, TILE), 0), iota((TILE, TILE), 1)
    identity = jnp.where(lane == row, 1.0, 0.0)
    powers = []
    for i in range(NB // TILE):
        part = slice(i * TILE, (i + 1) * TILE)
        powers.append(jnp.where(lane < row, -diag_ref[part, part].astype(F32), 0.0))
    inverses = [identity + p for p in powers]
    for _ in range(TILE.bit_length() - 2):
        powers = [mm3(p, p) for p in powers]
        inverses = [v + mm3(v, p) for v, p in zip(inverses, powers)]
    size = TILE
    while size < NB:
        none = jnp.zeros((size, size), F32)
        joined = []
        for i in range(0, len(inverses), 2):
            upper, lower = inverses[i], inverses[i + 1]
            between = diag_ref[(i + 1) * size : (i + 2) * size, i * size : (i + 1) * size]
            high, low = split(upper)
            corner = mm3(lower, mm(between, high) + mm(between, low))
            joined.append(
                jnp.concatenate(
                    [
                        jnp.concatenate([upper, none], axis=1),
                        jnp.concatenate([-corner, lower], axis=1),
                    ],
                    axis=0,
                )
            )
        inverses, size = joined, 2 * size
    high_ref[...], low_ref[...] = split(inverses[0])


def copies(pairs, sems):
    made = [pltpu.make_async_copy(source, target, sems.at[i]) for i, (source, target) in enumerate(pairs)]
    for copy in made:
        copy.start()
    return made


def first_solve_kernel(high_ref, low_ref, slot_ref, own_ref, *refs):
    parts, down_ref, outs = refs[:NZ], refs[NZ], refs[NZ + 1 : NZ + 1 + NX]
    gathered_ref, right_ref, select_ref, sems = refs[NZ + 1 + NX :]
    places = [slice(z * FLOCK, (z + 1) * FLOCK) for z in range(NZ)]
    pairs = [(part, gathered_ref.at[place]) for part, place in zip(parts, places)]
    moving = copies(pairs, sems)
    lane = iota((1, FLOCK), 1)
    for k in range(1, NX):
        lane = lane + jnp.where(iota((1, FLOCK), 1) >= k * CAP, GROUP - CAP, 0)
    for z, place in enumerate(places):
        select_ref[:, place] = hot(slot_ref[:, :1] == lane + z * CAP)
    for copy in moving:
        copy.wait()
    came = gathered_ref[places[1], :COLS]
    for place in places[2:]:
        came = came + gathered_ref[place, :COLS]
    down_ref[...] = jnp.where(lax.axis_index("row") == 0, own_ref[...], came)
    for i in range(0, NB, HALF):
        found = mm(select_ref[i : i + HALF], gathered_ref[...])
        high, low = split(found[:, :COLS] + found[:, COLS:])
        right_ref[i : i + HALF, :COLS] = high
        right_ref[i : i + HALF, COLS:] = low
    halves = []
    for i in range(0, NB, HALF):
        wide = mm(high_ref[i : i + HALF], right_ref[...])
        halves.append(wide[:, :COLS] + (wide[:, COLS:] + mm(low_ref[i : i + HALF], right_ref[:, :COLS])))
    left = iota((HALF, LANES), 1) < PART
    for x, ref in enumerate(outs):
        block = slice(x // 2 * LANES, (x // 2 + 1) * LANES)
        upper, lower = halves[0][:, block], halves[1][:, block]
        if x % 2 == 0:
            ref[...] = jnp.where(left, upper, pltpu.roll(lower, PART, 1)).astype(BF16)
        else:
            ref[...] = jnp.where(left, pltpu.roll(upper, PART, 1), lower).astype(BF16)


def both(value):
    return value + pltpu.roll(value, PART, 1)


def last_solve_kernel(high_ref, low_ref, slot_ref, down_ref, c0, c1, c2, c3, *refs):
    outs, (gathered_ref, select_ref, sems) = refs[:NZ], refs[NZ:]
    x = lax.axis_index("row") & (NX - 1)
    parts = [slice(s * GROUP, (s + 1) * GROUP) for s in range(NX)]
    pairs = [(ref, gathered_ref.at[part]) for ref, part in zip((c0, c1, c2, c3), parts)]
    moving = copies(pairs, sems)
    for s, part in enumerate(parts):
        first = ((x - s) & (NX - 1)) * GROUP
        select_ref[:, part] = hot(slot_ref[:, 2:3] == iota((1, GROUP), 1) + first)
    for copy in moving:
        copy.wait()
    high, low = split(both(mm(select_ref[...], gathered_ref[...])))
    parts = jnp.where(iota((NB, LANES), 1) < PART, high, low)
    solved = both(mm(high_ref[...], parts)) + mm(low_ref[...], high)
    left = iota((HALF, LANES), 1) < PART
    solved = jnp.where(left, solved[:HALF], solved[HALF:]).astype(BF16)
    for z, ref in enumerate(outs):
        ref[:HALF] = solved
        ref[HALF:] = down_ref[2 * z * FLOCK : 2 * (z + 1) * FLOCK]


def pass_on(solved, rows_ref, outs):
    x = lax.axis_index("row") & (NX - 1)
    for s, ref in enumerate(outs):
        start = pl.multiple_of(((x + s) & (NX - 1)) * CAP, CAP)
        rows = rows_ref[pl.ds(start, CAP), :]
        ref[:HALF] = solved
        ref[HALF : HALF + CAP] = rows[:, :LANES]
        ref[HALF + CAP :] = rows[:, LANES:]


def sum_of(refs, part):
    total = refs[0][part]
    for ref in refs[1:]:
        total = total + ref[part]
    return total


def relay_kernel(own_ref, down_ref, *refs):
    came, outs = refs[: NZ - 1], refs[NZ - 1 :]
    front = lax.axis_index("row") < NX
    pass_on(jnp.where(front, own_ref[...], sum_of(came, slice(None))), down_ref, outs)


def last_relay_kernel(own_ref, *refs):
    came, outs, rows_ref = refs[: NZ - 1], refs[NZ - 1 : -1], refs[-1]
    front = lax.axis_index("row") < NX
    message = jnp.where(front, own_ref[...], sum_of(came, slice(None)))
    rows_ref[:, :LANES] = message[HALF : HALF + FLOCK]
    rows_ref[:, LANES:] = message[HALF + FLOCK :]
    pass_on(message[:HALF], rows_ref, outs)


def receive(pieces, u_ref, down_ref):
    x = lax.axis_index("row") & (NX - 1)
    row, lane = iota((LANES, COLS), 0), iota((LANES, COLS), 1)
    above, below = jnp.zeros((HALF, COLS), F32), jnp.zeros((HALF, COLS), F32)
    for s, ref in enumerate(pieces):
        first = ((x - s) & (NX - 1)) * PART
        piece = ref[:HALF]
        above = above + mm(piece, hot((lane == first + row) & (row < PART)))
        below = below + mm(piece, hot((lane == first + row - PART) & (row >= PART)))
    u_ref[:HALF] = above.astype(BF16)
    u_ref[HALF:] = below.astype(BF16)
    down_ref[:CAP, :LANES] = sum_of(pieces, slice(HALF, HALF + CAP))
    down_ref[:CAP, LANES:] = sum_of(pieces, slice(HALF + CAP, HALF + 2 * CAP))
    down_ref[CAP:] = jnp.zeros((LANES - CAP, COLS), BF16)


def update(number, matrix_ref, to_ref, pieces, lower_refs, out_ref, scratch, then):
    u_ref, down_ref, rows_ref, lower_ref, rows_sem, lower_sem, out_sem = scratch
    me = lax.axis_index("row")
    count = 2 * NB // CHUNK
    each = count // len(lower_refs)

    def rows_of(i):
        return pl.ds(pl.multiple_of(i * CHUNK, CHUNK), CHUNK)

    def rows_copy(i):
        return pltpu.make_async_copy(matrix_ref.at[rows_of(i)], rows_ref.at[rows_of(i)], rows_sem.at[i])

    def out_copy(i):
        return pltpu.make_async_copy(rows_ref.at[rows_of(i)], out_ref.at[rows_of(i)], out_sem.at[i])

    for i in range(count):
        rows_copy(i).start()
        source = lower_refs[i // each].at[rows_of(i % each)]
        pltpu.make_async_copy(source, lower_ref.at[rows_of(i)], lower_sem.at[i]).start()
    receive(pieces, u_ref, down_ref)

    def step(i, carry):
        here = to_ref[2 * number + 1 : 2 * number + 2, :] == iota((CHUNK, LANES), 0) + i * CHUNK
        there = jnp.max(jnp.where(here, 1.0, 0.0), axis=1, keepdims=True) > 0.5
        moved = mm(hot(here), down_ref[...])
        rows_copy(i).wait()
        pltpu.make_async_copy(lower_ref.at[rows_of(i)], lower_ref.at[rows_of(i)], lower_sem.at[i]).wait()
        old = rows_ref[rows_of(i), :]
        new = jnp.where(there, moved, old) - mm(lower_ref[rows_of(i), :], u_ref[...])
        in_top = i < NB // CHUNK
        top = u_ref[rows_of(i & (NB // CHUNK - 1)), :].astype(F32)
        new = jnp.where(in_top & (me == number), top, jnp.where(in_top & (me < number), old, new))
        rows_ref[rows_of(i), :] = new
        out_copy(i).start()
        return then(i, new, carry)

    none = jnp.zeros((LANES, COLS), F32)
    carry = lax.fori_loop(0, count, step, (none, none), unroll=True)
    for i in range(count):
        out_copy(i).wait()
    return carry


def first_update_kernel(
    matrix_ref, to_ref, from_ref, m0, m1, m2, m3, top_ref, low_ref, out_ref, picked_ref, *scratch
):
    def then(i, rows, carry):
        high, low = pick(1, from_ref, i * CHUNK, rows)
        return carry[0] + high, carry[1] + low

    lowers = (top_ref, low_ref)
    high, low = update(0, matrix_ref, to_ref, (m0, m1, m2, m3), lowers, out_ref, scratch, then)
    picked_ref[:CAP] = high[:CAP].astype(BF16)
    picked_ref[CAP:] = low[:CAP].astype(BF16)


def last_update_kernel(matrix_ref, to_ref, m0, m1, m2, m3, lower_ref, out_ref, *scratch):
    then = lambda i, rows, carry: carry
    update(1, matrix_ref, to_ref, (m0, m1, m2, m3), (lower_ref,), out_ref, scratch, then)


def send(value, pairs):
    return lax.ppermute(value, "row", pairs)


def over_x(root_x, pieces):
    return [pieces[root_x]] + [
        send(pieces[(root_x + s) % NX], [(at(0, root_x), at(0, root_x + s))]) for s in range(1, NX)
    ]


def in_hbm(a):
    return pltpu.with_memory_space_constraint(a, pltpu.HBM)


def from_front(messages):
    return [messages[0]] + [
        send(messages[z], [(at(0, x), at(z, x)) for x in range(NX)]) for z in range(1, NZ)
    ]


def along_x(messages):
    return [messages[0]] + [
        send(messages[s], [(at(z, x), at(z, x + s)) for z in range(NZ) for x in range(NX)])
        for s in range(1, NX)
    ]


def local(slab, lower_first, lower_second, pivot_rows, displaced):
    row = lax.axis_index("row")
    matrix = slab.reshape(2 * NB, COLS)
    first, second = [p.reshape(2 * NB, p.shape[3]) for p in (lower_first, lower_second)]
    gather = lambda block: lax.all_gather(block, "col", axis=1, tiled=True)
    inverse = lambda d: call(inverse_kernel, [((NB, NB), BF16)] * 2, d, name="inverse", mib=32)
    picked_shape = ((2 * CAP, COLS), BF16)
    there, vmem = pl.BlockSpec(memory_space=pltpu.HBM), pl.BlockSpec(memory_space=pltpu.VMEM)
    block_of_top = pl.BlockSpec((NB, COLS), lambda i: (0, 0))
    update_scratch = [
        pltpu.VMEM((NB, COLS), BF16),
        pltpu.VMEM((LANES, COLS), BF16),
        pltpu.VMEM((2 * NB, COLS), F32),
        pltpu.VMEM((2 * NB, NB), BF16),
    ] + [pltpu.SemaphoreType.DMA((2 * NB // CHUNK,))] * 3
    relayed = [((HALF + 2 * CAP, LANES), BF16)] * NX
    rows = jnp.stack([pivot_rows, displaced], axis=1).reshape(4, NB)
    top = gather(first[:NB])
    rows = jnp.concatenate([rows, rows], axis=0)
    slot, order, pivots, targets = call(
        index_kernel,
        [((NB, LANES), I32), ((8, NB), I32), ((LANES, LANES), I32), ((8, LANES), I32)],
        rows,
        name="index",
    )
    (picked,) = call(pick_kernel, [picked_shape], matrix, pivots, name="pick")
    late, picked = lax.optimization_barrier((first, picked))
    low = gather(late[NB:])

    by_x = [picked] + [
        send(picked, [(at(z, x + s), at(z, x)) for z in range(NZ) for x in range(NX)]) for s in range(1, NX)
    ]
    joined, own_down, *messages = call(
        first_front_kernel,
        [((FLOCK, 2 * COLS), BF16), ((FLOCK, COLS), BF16)] + [((FLOCK, 2 * COLS), BF16)] * (NZ - 1),
        matrix,
        order,
        *by_x,
        name="front",
        in_specs=[block_of_top] + [vmem] * 5,
        grid=(1,),
    )
    parts = [joined] + [
        in_hbm(send(message, [(at(z, 0), at(0, 0)), (at(0, 0), at(z, 0))]))
        for z, message in enumerate(messages, 1)
    ]
    inverses, parts[-1] = lax.optimization_barrier((inverse(top), parts[-1]))
    own_down, *solved = call(
        first_solve_kernel,
        [((FLOCK, COLS), BF16)] + [((HALF, LANES), BF16)] * NX,
        *inverses,
        slot,
        own_down,
        *parts,
        name="solve",
        in_specs=[vmem] * 4 + [there] * NZ,
        scratch=[pltpu.VMEM((NX * GROUP, 2 * COLS), BF16), pltpu.VMEM((NB, 2 * COLS), BF16)]
        + [pltpu.VMEM((NB, NX * GROUP), BF16)]
        + [pltpu.SemaphoreType.DMA((NZ,))],
        mib=20,
    )
    block, solved = lax.optimization_barrier((second[:NB], solved))
    hops = [send(block, [(at(0, 1), at(0, 2))])]
    pieces = over_x(0, solved)
    hops[0], pieces[-1] = lax.optimization_barrier((hops[0], pieces[-1]))
    hops.append(send(hops[0], [(at(0, 2), at(0, 3))]))
    piece = pieces[0]
    for s in range(1, NX):
        piece = jnp.where(row == s, pieces[s], piece)
    came = from_front([piece] * NZ)
    hops[1], came[1] = lax.optimization_barrier((hops[1], came[1]))
    hops.append(send(hops[1], [(at(0, 3), at(0, 0))]))
    messages = call(relay_kernel, relayed, piece, own_down, *came[1:], name="relay")
    hops, messages = lax.optimization_barrier((hops, messages))
    spread = along_x(messages)
    block = jnp.where(row == 1, block, hops[0] + hops[1] + hops[2])
    block, late = lax.optimization_barrier((block, second))
    diag, lower = gather(block), gather(late)
    matrix, picked = call(
        first_update_kernel,
        [((2 * NB, COLS), F32), picked_shape],
        matrix,
        targets,
        pivots,
        *spread,
        in_hbm(top),
        in_hbm(low),
        name="update",
        scratch=update_scratch,
        mib=16,
        in_specs=[there] + [vmem] * 6 + [there] * 2,
        out_specs=[there, vmem],
    )

    came = [picked] + [send(picked, [(at(z, x), at(0, x)) for x in range(NX)]) for z in range(1, NZ)]
    order, came[3] = lax.optimization_barrier((order, came[3]))
    (downs,) = call(
        last_down_kernel,
        [((2 * NZ * FLOCK, LANES), BF16)],
        matrix,
        order,
        name="down",
        in_specs=[block_of_top, vmem],
        grid=(1,),
    )
    cuts = call(cut_kernel, [((GROUP, LANES), BF16)] * NX, *came, name="cut")
    cuts = [in_hbm(cut) for cut in along_x(cuts)]
    messages = call(
        last_solve_kernel,
        [((HALF + 2 * FLOCK, LANES), BF16)] * NZ,
        *inverse(diag),
        slot,
        downs,
        *cuts,
        name="solve",
        in_specs=[vmem] * 4 + [there] * NX,
        scratch=[pltpu.VMEM((NX * GROUP, LANES), BF16), pltpu.VMEM((NB, NX * GROUP), BF16)]
        + [pltpu.SemaphoreType.DMA((NX,))],
        mib=20,
    )
    relay_scratch = [pltpu.VMEM((FLOCK, COLS), BF16)]
    messages = call(last_relay_kernel, relayed, *from_front(messages), name="relay", scratch=relay_scratch)
    (matrix,) = call(
        last_update_kernel,
        [((2 * NB, COLS), F32)],
        matrix,
        targets,
        *along_x(messages),
        in_hbm(lower),
        name="update",
        scratch=update_scratch,
        mib=16,
        in_specs=[there] + [vmem] * 5 + [there],
        out_specs=[there],
    )
    return matrix.reshape(2, 1, NB, COLS)


def solution(mesh):
    placed = (
        P(None, "row", None, "col"),
        P(None, "row", None, "col"),
        P(None, "row", None, "col"),
        P(),
        P(),
    )
    return jax.shard_map(
        local, mesh=mesh, in_specs=placed, out_specs=P(None, "row", None, "col"), check_vma=False
    )
```

```python
import functools

import jax
import jax.numpy as jnp
from jax import lax
from jax.experimental import pallas as pl
from jax.experimental.pallas import tpu as pltpu
from jax.sharding import PartitionSpec as P

NB = 1024
CAP = 48
NX, NZ, NY = 4, 8, 4
TILE = 128
LANES = 128
CHUNK = 512
FLOCK = NX * CAP
HALF = NB // 2
GROUP = NZ * CAP
COLS = 256
PART = COLS // NX
BF16, F32, I32 = jnp.bfloat16, jnp.float32, jnp.int32


def at(z, x):
    return (z % NZ) * NX + x % NX


def mm(a, b):
    return jnp.dot(a, b, preferred_element_type=F32)


def mm_t(a, b):
    return lax.dot_general(a, b, (((0,), (0,)), ((), ())), preferred_element_type=F32)


def iota(shape, axis):
    return lax.broadcasted_iota(I32, shape, axis)


def hot(mask):
    return jnp.where(mask, 1.0, 0.0).astype(BF16)


def split(value):
    high = value.astype(BF16)
    return high, (value - high.astype(F32)).astype(BF16)


def call(kernel, outs, *args, name, scratch=(), mib=10, **blocks):
    size = lambda a: a.size * a.dtype.itemsize
    return pl.pallas_call(
        kernel,
        out_shape=[jax.ShapeDtypeStruct(s, d) for s, d in outs],
        scratch_shapes=list(scratch),
        compiler_params=pltpu.CompilerParams(vmem_limit_bytes=mib * 2**20),
        cost_estimate=pl.CostEstimate(
            flops=0, bytes_accessed=sum(size(a) for a in args), transcendentals=0
        ),
        name=name,
        **blocks,
    )(*args)


def copies(pairs, sems):
    made = [pltpu.make_async_copy(source, target, sems.at[i]) for i, (source, target) in enumerate(pairs)]
    for copy in made:
        copy.start()
    return made


def place_in(rows):
    return ((rows >> 15) << 10) | (rows & (NB - 1))


def owner_of(rows):
    return (rows >> 10) & 31


def x_major(owner, rank):
    return ((owner & (NX - 1)) * NZ + (owner >> 2)) * CAP + rank


def index_kernel(rows_ref, matrix_ref, slot_ref, order_ref, from_ref, to_ref, picked_ref, held_ref, sems):
    chunks = [pl.ds(i * CHUNK, CHUNK) for i in range(2 * NB // CHUNK)]
    moving = copies([(matrix_ref.at[chunk], held_ref.at[chunk]) for chunk in chunks], sems)
    me = lax.axis_index("row")
    cols = rows_ref[...].astype(F32).T.astype(I32)
    lane = iota((NB, LANES), 1)
    owners = jnp.zeros((NB, LANES), I32)
    for k in range(4):
        owners = jnp.where(lane >> 5 == k, owner_of(cols[:, k : k + 1]), owners)
    own = jnp.where(owners == (lane & 31), 1.0, 0.0)
    earlier = hot(iota((TILE, TILE), 1) < iota((TILE, TILE), 0))
    before, count = [], jnp.zeros((1, LANES), F32)
    for i in range(NB // TILE):
        part = own[i * TILE : (i + 1) * TILE]
        before.append((mm(earlier, part.astype(BF16)) + count) * part)
        count = count + jnp.sum(part, axis=0, keepdims=True)
    before = jnp.concatenate(before, axis=0)
    slots, lists = jnp.zeros((NB, LANES), I32), jnp.zeros((LANES, LANES), I32)
    row, line = iota((8, NB), 0), iota((LANES, LANES), 0)
    for k in range(4):
        owner = owner_of(cols[:, k : k + 1])
        rank = jnp.sum(jnp.where(lane >> 5 == k, before, 0.0), axis=1, keepdims=True).astype(I32)
        slots = jnp.where(lane == k, x_major(owner, rank), slots)
        mine = hot((owner == me) & (rank == lane) & (lane < CAP))
        place = place_in(rows_ref[k : k + 1, :])
        parts = jnp.where(row == 0, place >> 6, jnp.where(row == 1, place & 63, 1))
        found = mm(parts.astype(F32).astype(BF16), mine).astype(I32)
        places = jnp.where(found[2:3] > 0, found[:1] * 64 + found[1:2], -1)
        lists = jnp.where(line == k, places, lists)
    slot_ref[...] = slots
    order_ref[...] = slots.astype(F32).T[:8].astype(I32)
    to_ref[...] = lists[:8]
    from_ref[...] = lists.astype(F32).T.astype(I32)
    high = low = jnp.zeros((LANES, COLS), F32)
    for i, chunk in enumerate(chunks):
        moving[i].wait()
        some = pick(0, from_ref, i * CHUNK, held_ref[chunk])
        high, low = high + some[0], low + some[1]
    picked_ref[:CAP] = high[:CAP].astype(BF16)
    picked_ref[CAP:] = low[:CAP].astype(BF16)


def pick(number, from_ref, start, rows):
    select = hot(from_ref[:, 2 * number : 2 * number + 1] == iota((LANES, rows.shape[0]), 1) + start)
    high, low = split(rows)
    return mm(select, high), mm(select, low)


def down(number, z, top, order_ref):
    line = iota((FLOCK, 1), 0)
    slot = line + z * CAP
    for k in range(1, NX):
        slot = slot + jnp.where(line >= k * CAP, GROUP - CAP, 0)
    order = order_ref[2 * number + 1 : 2 * number + 2, :]
    return mm(hot(order == slot), top).astype(BF16)


def first_front_kernel(top_ref, order_ref, b0, b1, b2, b3, joined_ref, own_ref, *outs):
    for s, ref in enumerate((b0, b1, b2, b3)):
        joined_ref[s * CAP : (s + 1) * CAP, :COLS] = ref[:CAP]
        joined_ref[s * CAP : (s + 1) * CAP, COLS:] = ref[CAP:]
    own_ref[...] = jnp.zeros_like(own_ref)
    is_root = lax.axis_index("row") == 0

    @pl.when(is_root)
    def _():
        top = top_ref[...].astype(BF16)
        own_ref[...] = down(0, 0, top, order_ref)
        for z, ref in enumerate(outs):
            ref[:, :COLS] = down(0, z + 1, top, order_ref)
            ref[:, COLS:] = jnp.zeros((FLOCK, COLS), BF16)

    @pl.when(jnp.logical_not(is_root))
    def _():
        for ref in outs:
            ref[...] = joined_ref[...]


def last_down_kernel(top_ref, order_ref, out_ref):
    out_ref[...] = jnp.zeros_like(out_ref)

    @pl.when(lax.axis_index("row") == 1)
    def _():
        top = top_ref[...].astype(BF16)
        for z in range(NZ):
            rows = down(1, z, top, order_ref)
            out_ref[2 * z * FLOCK : (2 * z + 1) * FLOCK] = rows[:, :LANES]
            out_ref[(2 * z + 1) * FLOCK : (2 * z + 2) * FLOCK] = rows[:, LANES:]


def cut_kernel(*refs):
    picked, outs = refs[:NZ], refs[NZ:]
    x = lax.axis_index("row") & (NX - 1)
    high = jnp.concatenate([p[:CAP] for p in picked], axis=0)
    low = jnp.concatenate([p[CAP:] for p in picked], axis=0)
    row, lane = iota((COLS, LANES), 0), iota((COLS, LANES), 1)
    for s, ref in enumerate(outs):
        first = ((x + s) & (NX - 1)) * PART
        left = hot((row == first + lane) & (lane < PART))
        right = hot((row == first + lane - PART) & (lane >= PART))
        ref[...] = (mm(high, left) + mm(low, right)).astype(BF16)


def mm3(a, b):
    a_high, a_low = split(a)
    b_high, b_low = split(b)
    return mm(a_high, b_high) + (mm(a_high, b_low) + mm(a_low, b_high))


def inverse_kernel(diag_hbm, high_ref, low_ref, diag_ref, tile_ref, sems):
    count = NB // TILE
    parts = [pl.ds(i * TILE, TILE) for i in range(count)]
    pairs = [(diag_hbm.at[part, part], tile_ref.at[i]) for i, part in enumerate(parts)]
    moving = copies(pairs + [(diag_hbm, diag_ref)], sems)
    row, lane = iota((TILE, TILE), 0), iota((TILE, TILE), 1)
    identity = jnp.where(lane == row, 1.0, 0.0)
    powers = []
    for i in range(count):
        moving[i].wait()
        powers.append(jnp.where(lane < row, -tile_ref[i].astype(F32), 0.0))
    inverses = [identity + p for p in powers]
    for _ in range(TILE.bit_length() - 2):
        powers = [mm3(p, p) for p in powers]
        inverses = [v + mm3(v, p) for v, p in zip(inverses, powers)]
    size = TILE
    moving[count].wait()
    while size < NB:
        none = jnp.zeros((size, size), F32)
        joined = []
        for i in range(0, len(inverses), 2):
            upper, lower = inverses[i], inverses[i + 1]
            between = diag_ref[(i + 1) * size : (i + 2) * size, i * size : (i + 1) * size]
            high, low = split(upper)
            corner = mm3(lower, mm(between, high) + mm(between, low))
            joined.append(
                jnp.concatenate(
                    [
                        jnp.concatenate([upper, none], axis=1),
                        jnp.concatenate([-corner, lower], axis=1),
                    ],
                    axis=0,
                )
            )
        inverses, size = joined, 2 * size
    high_ref[...], low_ref[...] = split(inverses[0])


def first_solve_kernel(high_ref, low_ref, slot_ref, own_ref, *refs):
    parts, down_ref, outs = refs[:NZ], refs[NZ], refs[NZ + 1 : NZ + 1 + NX]
    gathered_ref, right_ref, select_ref, sems = refs[NZ + 1 + NX :]
    places = [slice(z * FLOCK, (z + 1) * FLOCK) for z in range(NZ)]
    pairs = [(part, gathered_ref.at[place]) for part, place in zip(parts[1:], places[1:])]
    moving = copies(pairs, sems)
    gathered_ref[places[0]] = parts[0][...]
    lane = iota((1, FLOCK), 1)
    for k in range(1, NX):
        lane = lane + jnp.where(iota((1, FLOCK), 1) >= k * CAP, GROUP - CAP, 0)
    for z, place in enumerate(places):
        select_ref[:, place] = hot(slot_ref[:, :1] == lane + z * CAP)
    for copy in moving:
        copy.wait()
    came = gathered_ref[places[1], :COLS]
    for place in places[2:]:
        came = came + gathered_ref[place, :COLS]
    down_ref[...] = jnp.where(lax.axis_index("row") == 0, own_ref[...], came)
    for i in range(0, NB, HALF):
        found = mm(select_ref[i : i + HALF], gathered_ref[...])
        high, low = split(found[:, :COLS] + found[:, COLS:])
        right_ref[i : i + HALF, :COLS] = high
        right_ref[i : i + HALF, COLS:] = low
    halves = []
    for i in range(0, NB, HALF):
        wide = mm(high_ref[i : i + HALF], right_ref[...])
        halves.append(wide[:, :COLS] + (wide[:, COLS:] + mm(low_ref[i : i + HALF], right_ref[:, :COLS])))
    left = iota((HALF, LANES), 1) < PART
    for x, ref in enumerate(outs):
        block = slice(x // 2 * LANES, (x // 2 + 1) * LANES)
        upper, lower = halves[0][:, block], halves[1][:, block]
        if x % 2 == 0:
            ref[...] = jnp.where(left, upper, pltpu.roll(lower, PART, 1)).astype(BF16)
        else:
            ref[...] = jnp.where(left, pltpu.roll(upper, PART, 1), lower).astype(BF16)


def both(value):
    return value + pltpu.roll(value, PART, 1)


def last_solve_kernel(high_ref, low_ref, slot_ref, down_ref, c0, c1, c2, c3, *refs):
    outs, (gathered_ref, select_ref, sems) = refs[:NZ], refs[NZ:]
    x = lax.axis_index("row") & (NX - 1)
    parts = [slice(s * GROUP, (s + 1) * GROUP) for s in range(NX)]
    pairs = [(ref, gathered_ref.at[part]) for ref, part in zip((c1, c2, c3), parts[1:])]
    moving = copies(pairs, sems)
    gathered_ref[parts[0]] = c0[...]
    for s, part in enumerate(parts):
        first = ((x - s) & (NX - 1)) * GROUP
        select_ref[:, part] = hot(slot_ref[:, 2:3] == iota((1, GROUP), 1) + first)
    for copy in moving:
        copy.wait()
    high, low = split(both(mm(select_ref[...], gathered_ref[...])))
    parts = jnp.where(iota((NB, LANES), 1) < PART, high, low)
    solved = both(mm(high_ref[...], parts)) + mm(low_ref[...], high)
    left = iota((HALF, LANES), 1) < PART
    solved = jnp.where(left, solved[:HALF], solved[HALF:]).astype(BF16)
    for z, ref in enumerate(outs):
        ref[:HALF] = solved
        ref[HALF:] = down_ref[2 * z * FLOCK : 2 * (z + 1) * FLOCK]


def pass_on(solved, rows_ref, outs):
    x = lax.axis_index("row") & (NX - 1)
    for s, ref in enumerate(outs):
        start = pl.multiple_of(((x + s) & (NX - 1)) * CAP, CAP)
        rows = rows_ref[pl.ds(start, CAP), :]
        ref[:HALF] = solved
        ref[HALF : HALF + CAP] = rows[:, :LANES]
        ref[HALF + CAP :] = rows[:, LANES:]


def sum_of(refs, part):
    total = refs[0][part]
    for ref in refs[1:]:
        total = total + ref[part]
    return total


def relay_kernel(own_ref, down_ref, *refs):
    came, outs = refs[: NZ - 1], refs[NZ - 1 :]
    front = lax.axis_index("row") < NX
    pass_on(jnp.where(front, own_ref[...], sum_of(came, slice(None))), down_ref, outs)


def last_relay_kernel(own_ref, *refs):
    came, outs, rows_ref = refs[: NZ - 1], refs[NZ - 1 : -1], refs[-1]
    front = lax.axis_index("row") < NX
    message = jnp.where(front, own_ref[...], sum_of(came, slice(None)))
    rows_ref[:, :LANES] = message[HALF : HALF + FLOCK]
    rows_ref[:, LANES:] = message[HALF + FLOCK :]
    pass_on(message[:HALF], rows_ref, outs)


def receive(pieces, u_ref, down_ref):
    x = lax.axis_index("row") & (NX - 1)
    row, lane = iota((LANES, COLS), 0), iota((LANES, COLS), 1)
    above, below = jnp.zeros((HALF, COLS), F32), jnp.zeros((HALF, COLS), F32)
    for s, ref in enumerate(pieces):
        first = ((x - s) & (NX - 1)) * PART
        piece = ref[:HALF]
        above = above + mm(piece, hot((lane == first + row) & (row < PART)))
        below = below + mm(piece, hot((lane == first + row - PART) & (row >= PART)))
    u_ref[:HALF] = above.astype(BF16)
    u_ref[HALF:] = below.astype(BF16)
    down_ref[:CAP, :LANES] = sum_of(pieces, slice(HALF, HALF + CAP))
    down_ref[:CAP, LANES:] = sum_of(pieces, slice(HALF + CAP, HALF + 2 * CAP))
    down_ref[CAP:] = jnp.zeros((LANES - CAP, COLS), BF16)


def update(number, matrix_ref, to_ref, pieces, lower_refs, out_ref, scratch):
    u_ref, down_ref, rows_ref, lower_ref, rows_sem, lower_sem, out_sem = scratch
    me = lax.axis_index("row")
    count = 2 * NB // CHUNK
    each = count // len(lower_refs)

    def rows_of(i):
        return pl.ds(pl.multiple_of(i * CHUNK, CHUNK), CHUNK)

    def rows_copy(i):
        return pltpu.make_async_copy(matrix_ref.at[rows_of(i)], rows_ref.at[rows_of(i)], rows_sem.at[i])

    def out_copy(i):
        return pltpu.make_async_copy(rows_ref.at[rows_of(i)], out_ref.at[rows_of(i)], out_sem.at[i])

    for i in range(count):
        rows_copy(i).start()
        source = lower_refs[i // each].at[rows_of(i % each)]
        pltpu.make_async_copy(source, lower_ref.at[rows_of(i)], lower_sem.at[i]).start()
    receive(pieces, u_ref, down_ref)

    def step(i, carry):
        here = to_ref[2 * number + 1 : 2 * number + 2, :] == iota((CHUNK, LANES), 0) + i * CHUNK
        there = jnp.max(jnp.where(here, 1.0, 0.0), axis=1, keepdims=True) > 0.5
        moved = mm(hot(here), down_ref[...])
        rows_copy(i).wait()
        pltpu.make_async_copy(lower_ref.at[rows_of(i)], lower_ref.at[rows_of(i)], lower_sem.at[i]).wait()
        old = rows_ref[rows_of(i), :]
        new = jnp.where(there, moved, old) - mm(lower_ref[rows_of(i), :], u_ref[...])
        in_top = i < NB // CHUNK
        top = u_ref[rows_of(i & (NB // CHUNK - 1)), :].astype(F32)
        new = jnp.where(in_top & (me == number), top, jnp.where(in_top & (me < number), old, new))
        rows_ref[rows_of(i), :] = new
        out_copy(i).start()
        return carry

    lax.fori_loop(0, count, step, 0, unroll=True)
    for i in range(count):
        out_copy(i).wait()


def update_kernel(number, matrix_ref, to_ref, m0, m1, m2, m3, *refs):
    lowers, out_ref, scratch = refs[: 2 - number], refs[2 - number], refs[3 - number :]
    update(number, matrix_ref, to_ref, (m0, m1, m2, m3), lowers, out_ref, scratch)


def ahead_kernel(from_ref, matrix_ref, top_ref, low_ref, rows_ref, panel_ref, held_ref, lower_ref, sems):
    count = 2 * NB // CHUNK
    pairs = []
    for i in range(count):
        chunk, inner = pl.ds(i * CHUNK, CHUNK), pl.ds(i * CHUNK % NB, CHUNK)
        pairs.append((matrix_ref.at[chunk], held_ref.at[chunk]))
        pairs.append(((top_ref, low_ref)[i * CHUNK // NB].at[inner], lower_ref.at[chunk]))
    moving = copies(pairs, sems)
    rows, panel = jnp.zeros((LANES, COLS), F32), jnp.zeros((LANES, NB), F32)
    for i in range(count):
        chunk = pl.ds(i * CHUNK, CHUNK)
        select = hot(from_ref[:, 2:3] == iota((LANES, CHUNK), 1) + i * CHUNK)
        moving[2 * i].wait()
        high, low = split(held_ref[chunk])
        rows = rows + (mm(select, high) + mm(select, low))
        moving[2 * i + 1].wait()
        panel = panel + mm(select, lower_ref[chunk])
    rows_ref[...] = rows
    panel_ref[...] = panel.astype(BF16)


def pivots_kernel(from_ref, to_ref, rows_ref, panel_ref, m0, m1, m2, m3, picked_ref, u_ref, down_ref):
    receive((m0, m1, m2, m3), u_ref, down_ref)
    same = jnp.where(from_ref[:, 2:3] == to_ref[1:2, :], 1.0, 0.0)
    moved = jnp.max(same, axis=1, keepdims=True) > 0.5
    rows = jnp.where(moved, mm(same.astype(BF16), down_ref[...]), rows_ref[...])
    high, low = split(rows - mm(panel_ref[...], u_ref[...]))
    picked_ref[:CAP] = high[:CAP]
    picked_ref[CAP:] = low[:CAP]


def send(value, pairs):
    return lax.ppermute(value, "row", pairs)


def over_x(root_x, pieces):
    return [pieces[root_x]] + [
        send(pieces[(root_x + s) % NX], [(at(0, root_x), at(0, root_x + s))]) for s in range(1, NX)
    ]


def in_hbm(a):
    return pltpu.with_memory_space_constraint(a, pltpu.HBM)


def from_front(messages):
    return [messages[0]] + [
        send(messages[z], [(at(0, x), at(z, x)) for x in range(NX)]) for z in range(1, NZ)
    ]


def along_x(messages):
    return [messages[0]] + [
        send(messages[s], [(at(z, x), at(z, x + s)) for z in range(NZ) for x in range(NX)])
        for s in range(1, NX)
    ]


def local(slab, lower_first, lower_second, pivot_rows, displaced):
    row = lax.axis_index("row")
    matrix = slab.reshape(2 * NB, COLS)
    first, second = [p.reshape(2 * NB, p.shape[3]) for p in (lower_first, lower_second)]
    gather = lambda block: lax.all_gather(block, "col", axis=1, tiled=True)
    picked_shape = ((2 * CAP, COLS), BF16)
    there, vmem = pl.BlockSpec(memory_space=pltpu.HBM), pl.BlockSpec(memory_space=pltpu.VMEM)
    block_of_top = pl.BlockSpec((NB, COLS), lambda i: (0, 0))
    update_scratch = [
        pltpu.VMEM((NB, COLS), BF16),
        pltpu.VMEM((LANES, COLS), BF16),
        pltpu.VMEM((2 * NB, COLS), F32),
        pltpu.VMEM((2 * NB, NB), BF16),
    ] + [pltpu.SemaphoreType.DMA((2 * NB // CHUNK,))] * 3
    inverse = lambda d: call(
        inverse_kernel,
        [((NB, NB), BF16)] * 2,
        in_hbm(d),
        name="inverse",
        in_specs=[there],
        scratch=[pltpu.VMEM((NB, NB), BF16), pltpu.VMEM((NB // TILE, TILE, TILE), BF16)]
        + [pltpu.SemaphoreType.DMA((NB // TILE + 1,))],
        mib=24,
    )
    relayed = [((HALF + 2 * CAP, LANES), BF16)] * NX
    rows = jnp.stack([pivot_rows, displaced], axis=1).reshape(4, NB)
    top = gather(first[:NB])
    rows = jnp.concatenate([rows, rows], axis=0)
    slot, order, pivots, targets, picked = call(
        index_kernel,
        [((NB, LANES), I32), ((8, NB), I32), ((LANES, LANES), I32), ((8, LANES), I32), picked_shape],
        rows,
        in_hbm(matrix),
        name="index",
        in_specs=[vmem, there],
        scratch=[pltpu.VMEM((2 * NB, COLS), F32), pltpu.SemaphoreType.DMA((2 * NB // CHUNK,))],
    )
    late, picked = lax.optimization_barrier((first, picked))
    low = gather(late[NB:])

    by_x = [picked] + [
        send(picked, [(at(z, x + s), at(z, x)) for z in range(NZ) for x in range(NX)]) for s in range(1, NX)
    ]
    joined, own_down, *messages = call(
        first_front_kernel,
        [((FLOCK, 2 * COLS), BF16), ((FLOCK, COLS), BF16)] + [((FLOCK, 2 * COLS), BF16)] * (NZ - 1),
        matrix,
        order,
        *by_x,
        name="front",
        in_specs=[block_of_top] + [vmem] * 5,
        grid=(1,),
    )
    parts = [joined] + [
        in_hbm(send(message, [(at(z, 0), at(0, 0)), (at(0, 0), at(z, 0))]))
        for z, message in enumerate(messages, 1)
    ]
    inverses, parts[-1] = lax.optimization_barrier((inverse(top), parts[-1]))
    own_down, *solved = call(
        first_solve_kernel,
        [((FLOCK, COLS), BF16)] + [((HALF, LANES), BF16)] * NX,
        *inverses,
        slot,
        own_down,
        *parts,
        name="solve",
        in_specs=[vmem] * 5 + [there] * (NZ - 1),
        scratch=[pltpu.VMEM((NX * GROUP, 2 * COLS), BF16), pltpu.VMEM((NB, 2 * COLS), BF16)]
        + [pltpu.VMEM((NB, NX * GROUP), BF16)]
        + [pltpu.SemaphoreType.DMA((NZ,))],
        mib=20,
    )
    block, solved = lax.optimization_barrier((second[:NB], solved))
    hops = [send(block, [(at(0, 1), at(0, 2))])]
    pieces = over_x(0, solved)
    hops[0], pieces[-1] = lax.optimization_barrier((hops[0], pieces[-1]))
    hops.append(send(hops[0], [(at(0, 2), at(0, 3))]))
    piece = pieces[0]
    for s in range(1, NX):
        piece = jnp.where(row == s, pieces[s], piece)
    came = from_front([piece] * NZ)
    hops[1], came[1] = lax.optimization_barrier((hops[1], came[1]))
    hops.append(send(hops[1], [(at(0, 3), at(0, 0))]))
    messages = call(relay_kernel, relayed, piece, own_down, *came[1:], name="relay")
    hops, messages = lax.optimization_barrier((hops, messages))
    spread = along_x(messages)
    block = jnp.where(row == 1, block, hops[0] + hops[1] + hops[2])
    block, late = lax.optimization_barrier((block, second))
    diag, lower = gather(block), gather(late)
    top, low = in_hbm(top), in_hbm(low)
    ready, late = lax.optimization_barrier((pivots, spread[0]))
    ahead = call(
        ahead_kernel,
        [((LANES, COLS), F32), ((LANES, NB), BF16)],
        ready,
        in_hbm(matrix),
        top,
        low,
        name="ahead",
        in_specs=[vmem] + [there] * 3,
        scratch=update_scratch[2:4] + [pltpu.SemaphoreType.DMA((4 * NB // CHUNK,))],
        mib=16,
    )
    (picked,) = call(
        pivots_kernel,
        [picked_shape],
        pivots,
        targets,
        *ahead,
        *spread,
        name="pivots",
        scratch=update_scratch[:2],
    )
    came = [picked] + [send(picked, [(at(z, x), at(0, x)) for x in range(NX)]) for z in range(1, NZ)]
    (matrix,) = call(
        functools.partial(update_kernel, 0),
        [((2 * NB, COLS), F32)],
        matrix,
        targets,
        *spread,
        top,
        low,
        name="update",
        scratch=update_scratch,
        mib=16,
        in_specs=[there] + [vmem] * 5 + [there] * 2,
        out_specs=[there],
    )
    matrix, came[-1] = lax.optimization_barrier((matrix, came[-1]))
    order, came[3] = lax.optimization_barrier((order, came[3]))
    (downs,) = call(
        last_down_kernel,
        [((2 * NZ * FLOCK, LANES), BF16)],
        matrix,
        order,
        name="down",
        in_specs=[block_of_top, vmem],
        grid=(1,),
    )
    cuts = call(cut_kernel, [((GROUP, LANES), BF16)] * NX, *came, name="cut")
    cuts = along_x(cuts)
    cuts = cuts[:1] + [in_hbm(cut) for cut in cuts[1:]]
    messages = call(
        last_solve_kernel,
        [((HALF + 2 * FLOCK, LANES), BF16)] * NZ,
        *inverse(diag),
        slot,
        downs,
        *cuts,
        name="solve",
        in_specs=[vmem] * 5 + [there] * (NX - 1),
        scratch=[pltpu.VMEM((NX * GROUP, LANES), BF16), pltpu.VMEM((NB, NX * GROUP), BF16)]
        + [pltpu.SemaphoreType.DMA((NX,))],
        mib=20,
    )
    relay_scratch = [pltpu.VMEM((FLOCK, COLS), BF16)]
    messages = call(last_relay_kernel, relayed, *from_front(messages), name="relay", scratch=relay_scratch)
    (matrix,) = call(
        functools.partial(update_kernel, 1),
        [((2 * NB, COLS), F32)],
        matrix,
        targets,
        *along_x(messages),
        in_hbm(lower),
        name="update",
        scratch=update_scratch,
        mib=16,
        in_specs=[there] + [vmem] * 5 + [there],
        out_specs=[there],
    )
    return matrix.reshape(2, 1, NB, COLS)


def solution(mesh):
    placed = (
        P(None, "row", None, "col"),
        P(None, "row", None, "col"),
        P(None, "row", None, "col"),
        P(),
        P(),
    )
    return jax.shard_map(
        local, mesh=mesh, in_specs=placed, out_specs=P(None, "row", None, "col"), check_vma=False
    )
```

```python
import functools

import jax
import jax.numpy as jnp
from jax import lax
from jax.experimental import pallas as pl
from jax.experimental.pallas import tpu as pltpu
from jax.sharding import PartitionSpec as P

NB = 1024
CAP = 48
NX, NZ, NY = 4, 8, 4
TILE = 128
LANES = 128
CHUNK = 512
FLOCK = NX * CAP
HALF = NB // 2
GROUP = NZ * CAP
COLS = 256
PART = COLS // NX
BF16, F32, I32 = jnp.bfloat16, jnp.float32, jnp.int32


def at(z, x):
    return (z % NZ) * NX + x % NX


def mm(a, b):
    return jnp.dot(a, b, preferred_element_type=F32)


def mm_t(a, b):
    return lax.dot_general(a, b, (((0,), (0,)), ((), ())), preferred_element_type=F32)


def iota(shape, axis):
    return lax.broadcasted_iota(I32, shape, axis)


def hot(mask):
    return jnp.where(mask, 1.0, 0.0).astype(BF16)


def split(value):
    high = value.astype(BF16)
    return high, (value - high.astype(F32)).astype(BF16)


def call(kernel, outs, *args, name, scratch=(), mib=10, **blocks):
    size = lambda a: a.size * a.dtype.itemsize
    return pl.pallas_call(
        kernel,
        out_shape=[jax.ShapeDtypeStruct(s, d) for s, d in outs],
        scratch_shapes=list(scratch),
        compiler_params=pltpu.CompilerParams(vmem_limit_bytes=mib * 2**20),
        cost_estimate=pl.CostEstimate(
            flops=0, bytes_accessed=sum(size(a) for a in args), transcendentals=0
        ),
        name=name,
        **blocks,
    )(*args)


def copies(pairs, sems):
    made = [pltpu.make_async_copy(source, target, sems.at[i]) for i, (source, target) in enumerate(pairs)]
    for copy in made:
        copy.start()
    return made


def place_in(rows):
    return ((rows >> 15) << 10) | (rows & (NB - 1))


def owner_of(rows):
    return (rows >> 10) & 31


def x_major(owner, rank):
    return ((owner & (NX - 1)) * NZ + (owner >> 2)) * CAP + rank


def index_kernel(rows_ref, matrix_ref, slot_ref, order_ref, from_ref, to_ref, picked_ref, held_ref, sems):
    chunks = [pl.ds(i * CHUNK, CHUNK) for i in range(2 * NB // CHUNK)]
    moving = copies([(matrix_ref.at[chunk], held_ref.at[chunk]) for chunk in chunks], sems)
    me = lax.axis_index("row")
    cols = rows_ref[...].astype(F32).T.astype(I32)
    lane = iota((NB, LANES), 1)
    owners = jnp.zeros((NB, LANES), I32)
    for k in range(4):
        owners = jnp.where(lane >> 5 == k, owner_of(cols[:, k : k + 1]), owners)
    own = jnp.where(owners == (lane & 31), 1.0, 0.0)
    earlier = hot(iota((TILE, TILE), 1) < iota((TILE, TILE), 0))
    before, count = [], jnp.zeros((1, LANES), F32)
    for i in range(NB // TILE):
        part = own[i * TILE : (i + 1) * TILE]
        before.append((mm(earlier, part.astype(BF16)) + count) * part)
        count = count + jnp.sum(part, axis=0, keepdims=True)
    before = jnp.concatenate(before, axis=0)
    slots, lists = jnp.zeros((NB, LANES), I32), jnp.zeros((LANES, LANES), I32)
    row, line = iota((8, NB), 0), iota((LANES, LANES), 0)
    for k in range(4):
        owner = owner_of(cols[:, k : k + 1])
        rank = jnp.sum(jnp.where(lane >> 5 == k, before, 0.0), axis=1, keepdims=True).astype(I32)
        slots = jnp.where(lane == k, x_major(owner, rank), slots)
        mine = hot((owner == me) & (rank == lane) & (lane < CAP))
        place = place_in(rows_ref[k : k + 1, :])
        parts = jnp.where(row == 0, place >> 6, jnp.where(row == 1, place & 63, 1))
        found = mm(parts.astype(F32).astype(BF16), mine).astype(I32)
        places = jnp.where(found[2:3] > 0, found[:1] * 64 + found[1:2], -1)
        lists = jnp.where(line == k, places, lists)
    slot_ref[...] = slots
    order_ref[...] = slots.astype(F32).T[:8].astype(I32)
    to_ref[...] = lists[:8]
    from_ref[...] = lists.astype(F32).T.astype(I32)
    high = low = jnp.zeros((LANES, COLS), F32)
    for i, chunk in enumerate(chunks):
        moving[i].wait()
        some = pick(0, from_ref, i * CHUNK, held_ref[chunk])
        high, low = high + some[0], low + some[1]
    picked_ref[:CAP] = high[:CAP].astype(BF16)
    picked_ref[CAP:] = low[:CAP].astype(BF16)


def pick(number, from_ref, start, rows):
    select = hot(from_ref[:, 2 * number : 2 * number + 1] == iota((LANES, rows.shape[0]), 1) + start)
    high, low = split(rows)
    return mm(select, high), mm(select, low)


def down(number, z, top, order_ref):
    line = iota((FLOCK, 1), 0)
    slot = line + z * CAP
    for k in range(1, NX):
        slot = slot + jnp.where(line >= k * CAP, GROUP - CAP, 0)
    order = order_ref[2 * number + 1 : 2 * number + 2, :]
    return mm(hot(order == slot), top).astype(BF16)


def first_front_kernel(top_ref, order_ref, b0, b1, b2, b3, joined_ref, own_ref, *outs):
    for s, ref in enumerate((b0, b1, b2, b3)):
        joined_ref[s * CAP : (s + 1) * CAP, :COLS] = ref[:CAP]
        joined_ref[s * CAP : (s + 1) * CAP, COLS:] = ref[CAP:]
    own_ref[...] = jnp.zeros_like(own_ref)
    is_root = lax.axis_index("row") == 0

    @pl.when(is_root)
    def _():
        top = top_ref[...].astype(BF16)
        own_ref[...] = down(0, 0, top, order_ref)
        for z, ref in enumerate(outs):
            ref[:, :COLS] = down(0, z + 1, top, order_ref)
            ref[:, COLS:] = jnp.zeros((FLOCK, COLS), BF16)

    @pl.when(jnp.logical_not(is_root))
    def _():
        for ref in outs:
            ref[...] = joined_ref[...]


def last_down_kernel(top_ref, order_ref, out_ref):
    out_ref[...] = jnp.zeros_like(out_ref)

    @pl.when(lax.axis_index("row") == 1)
    def _():
        top = top_ref[...].astype(BF16)
        for z in range(NZ):
            rows = down(1, z, top, order_ref)
            out_ref[2 * z * FLOCK : (2 * z + 1) * FLOCK] = rows[:, :LANES]
            out_ref[(2 * z + 1) * FLOCK : (2 * z + 2) * FLOCK] = rows[:, LANES:]


def cut_kernel(*refs):
    picked, outs = refs[:NZ], refs[NZ:]
    x = lax.axis_index("row") & (NX - 1)
    high = jnp.concatenate([p[:CAP] for p in picked], axis=0)
    low = jnp.concatenate([p[CAP:] for p in picked], axis=0)
    row, lane = iota((COLS, LANES), 0), iota((COLS, LANES), 1)
    for s, ref in enumerate(outs):
        first = ((x + s) & (NX - 1)) * PART
        left = hot((row == first + lane) & (lane < PART))
        right = hot((row == first + lane - PART) & (lane >= PART))
        ref[...] = (mm(high, left) + mm(low, right)).astype(BF16)


def mm3(a, b):
    a_high, a_low = split(a)
    b_high, b_low = split(b)
    return mm(a_high, b_high) + (mm(a_high, b_low) + mm(a_low, b_high))


def inverse_kernel(diag_hbm, high_ref, low_ref, below_ref, diag_ref, tile_ref, sems):
    count = NB // TILE
    parts = [pl.ds(i * TILE, TILE) for i in range(count)]
    pairs = [(diag_hbm.at[part, part], tile_ref.at[i]) for i, part in enumerate(parts)]
    moving = copies(pairs + [(diag_hbm, diag_ref)], sems)
    row, lane = iota((TILE, TILE), 0), iota((TILE, TILE), 1)
    identity = jnp.where(lane == row, 1.0, 0.0)
    powers = []
    for i in range(count):
        moving[i].wait()
        powers.append(jnp.where(lane < row, -tile_ref[i].astype(F32), 0.0))
    inverses = [identity + p for p in powers]
    for _ in range(TILE.bit_length() - 2):
        powers = [mm3(p, p) for p in powers]
        inverses = [v + mm3(v, p) for v, p in zip(inverses, powers)]
    size = TILE
    moving[count].wait()
    below_ref[...] = diag_ref[HALF:, :HALF]
    while size < HALF:
        none = jnp.zeros((size, size), F32)
        joined = []
        for i in range(0, len(inverses), 2):
            upper, lower = inverses[i], inverses[i + 1]
            between = diag_ref[(i + 1) * size : (i + 2) * size, i * size : (i + 1) * size]
            high, low = split(upper)
            corner = mm3(lower, mm(between, high) + mm(between, low))
            joined.append(
                jnp.concatenate(
                    [
                        jnp.concatenate([upper, none], axis=1),
                        jnp.concatenate([-corner, lower], axis=1),
                    ],
                    axis=0,
                )
            )
        inverses, size = joined, 2 * size
    for i, value in enumerate(inverses):
        part = slice(i * HALF, (i + 1) * HALF)
        high_ref[part], low_ref[part] = split(value)


def first_solve_kernel(high_ref, low_ref, below_ref, slot_ref, own_ref, *refs):
    parts, down_ref, outs = refs[:NZ], refs[NZ], refs[NZ + 1 : NZ + 1 + NX]
    gathered_ref, right_ref, select_ref, sems = refs[NZ + 1 + NX :]
    places = [slice(z * FLOCK, (z + 1) * FLOCK) for z in range(NZ)]
    pairs = [(part, gathered_ref.at[place]) for part, place in zip(parts[1:], places[1:])]
    moving = copies(pairs, sems)
    gathered_ref[places[0]] = parts[0][...]
    lane = iota((1, FLOCK), 1)
    for k in range(1, NX):
        lane = lane + jnp.where(iota((1, FLOCK), 1) >= k * CAP, GROUP - CAP, 0)
    for z, place in enumerate(places):
        select_ref[:, place] = hot(slot_ref[:, :1] == lane + z * CAP)
    for copy in moving:
        copy.wait()
    came = gathered_ref[places[1], :COLS]
    for place in places[2:]:
        came = came + gathered_ref[place, :COLS]
    down_ref[...] = jnp.where(lax.axis_index("row") == 0, own_ref[...], came)

    def wide_parts(place, value):
        part = slice(place * HALF, (place + 1) * HALF)
        right_ref[part, :COLS], right_ref[part, COLS:] = split(value)
        return right_ref[part]

    def fold(wide):
        return wide[:, :COLS] + wide[:, COLS:]

    found = [fold(mm(select_ref[i : i + HALF], gathered_ref[...])) for i in range(0, NB, HALF)]
    first = wide_parts(0, found[0])
    upper = fold(mm(high_ref[:HALF], first)) + mm(low_ref[:HALF], first[:, :COLS])
    second = wide_parts(2, found[1] - fold(mm(below_ref[...], wide_parts(1, upper))))
    lower = fold(mm(high_ref[HALF:], second)) + mm(low_ref[HALF:], second[:, :COLS])
    halves = [upper, lower]
    left = iota((HALF, LANES), 1) < PART
    for x, ref in enumerate(outs):
        block = slice(x // 2 * LANES, (x // 2 + 1) * LANES)
        upper, lower = halves[0][:, block], halves[1][:, block]
        if x % 2 == 0:
            ref[...] = jnp.where(left, upper, pltpu.roll(lower, PART, 1)).astype(BF16)
        else:
            ref[...] = jnp.where(left, pltpu.roll(upper, PART, 1), lower).astype(BF16)


def both(value):
    return value + pltpu.roll(value, PART, 1)


def last_solve_kernel(high_ref, low_ref, below_ref, slot_ref, down_ref, c0, c1, c2, c3, *refs):
    outs, (gathered_ref, select_ref, sems) = refs[:NZ], refs[NZ:]
    x = lax.axis_index("row") & (NX - 1)
    parts = [slice(s * GROUP, (s + 1) * GROUP) for s in range(NX)]
    pairs = [(ref, gathered_ref.at[part]) for ref, part in zip((c1, c2, c3), parts[1:])]
    moving = copies(pairs, sems)
    gathered_ref[parts[0]] = c0[...]
    for s, part in enumerate(parts):
        first = ((x - s) & (NX - 1)) * GROUP
        select_ref[:, part] = hot(slot_ref[:, 2:3] == iota((1, GROUP), 1) + first)
    for copy in moving:
        copy.wait()
    left = iota((HALF, LANES), 1) < PART
    halves = []
    for i in range(0, NB, HALF):
        found = both(mm(select_ref[i : i + HALF], gathered_ref[...]))
        if i > 0:
            high, low = split(halves[0])
            found = found - both(mm(below_ref[...], jnp.where(left, high, low)))
        high, low = split(found)
        wide = both(mm(high_ref[i : i + HALF], jnp.where(left, high, low)))
        halves.append(wide + mm(low_ref[i : i + HALF], high))
    solved = jnp.where(left, halves[0], halves[1]).astype(BF16)
    for z, ref in enumerate(outs):
        ref[:HALF] = solved
        ref[HALF:] = down_ref[2 * z * FLOCK : 2 * (z + 1) * FLOCK]


def pass_on(solved, rows_ref, outs):
    x = lax.axis_index("row") & (NX - 1)
    for s, ref in enumerate(outs):
        start = pl.multiple_of(((x + s) & (NX - 1)) * CAP, CAP)
        rows = rows_ref[pl.ds(start, CAP), :]
        ref[:HALF] = solved
        ref[HALF : HALF + CAP] = rows[:, :LANES]
        ref[HALF + CAP :] = rows[:, LANES:]


def sum_of(refs, part):
    total = refs[0][part]
    for ref in refs[1:]:
        total = total + ref[part]
    return total


def relay_kernel(own_ref, down_ref, *refs):
    came, outs = refs[: NZ - 1], refs[NZ - 1 :]
    front = lax.axis_index("row") < NX
    pass_on(jnp.where(front, own_ref[...], sum_of(came, slice(None))), down_ref, outs)


def last_relay_kernel(own_ref, *refs):
    came, outs, rows_ref = refs[: NZ - 1], refs[NZ - 1 : -1], refs[-1]
    front = lax.axis_index("row") < NX
    message = jnp.where(front, own_ref[...], sum_of(came, slice(None)))
    rows_ref[:, :LANES] = message[HALF : HALF + FLOCK]
    rows_ref[:, LANES:] = message[HALF + FLOCK :]
    pass_on(message[:HALF], rows_ref, outs)


def receive(pieces, u_ref, down_ref):
    x = lax.axis_index("row") & (NX - 1)
    row, lane = iota((LANES, COLS), 0), iota((LANES, COLS), 1)
    above, below = jnp.zeros((HALF, COLS), F32), jnp.zeros((HALF, COLS), F32)
    for s, ref in enumerate(pieces):
        first = ((x - s) & (NX - 1)) * PART
        piece = ref[:HALF]
        above = above + mm(piece, hot((lane == first + row) & (row < PART)))
        below = below + mm(piece, hot((lane == first + row - PART) & (row >= PART)))
    u_ref[:HALF] = above.astype(BF16)
    u_ref[HALF:] = below.astype(BF16)
    down_ref[:CAP, :LANES] = sum_of(pieces, slice(HALF, HALF + CAP))
    down_ref[:CAP, LANES:] = sum_of(pieces, slice(HALF + CAP, HALF + 2 * CAP))
    down_ref[CAP:] = jnp.zeros((LANES - CAP, COLS), BF16)


def update(number, matrix_ref, to_ref, pieces, lower_refs, out_ref, scratch):
    u_ref, down_ref, rows_ref, lower_ref, rows_sem, lower_sem, out_sem = scratch
    me = lax.axis_index("row")
    count = 2 * NB // CHUNK
    each = count // len(lower_refs)

    def rows_of(i):
        return pl.ds(pl.multiple_of(i * CHUNK, CHUNK), CHUNK)

    def rows_copy(i):
        return pltpu.make_async_copy(matrix_ref.at[rows_of(i)], rows_ref.at[rows_of(i)], rows_sem.at[i])

    def out_copy(i):
        return pltpu.make_async_copy(rows_ref.at[rows_of(i)], out_ref.at[rows_of(i)], out_sem.at[i])

    for i in range(count):
        rows_copy(i).start()
        source = lower_refs[i // each].at[rows_of(i % each)]
        pltpu.make_async_copy(source, lower_ref.at[rows_of(i)], lower_sem.at[i]).start()
    receive(pieces, u_ref, down_ref)

    def step(i, carry):
        here = to_ref[2 * number + 1 : 2 * number + 2, :] == iota((CHUNK, LANES), 0) + i * CHUNK
        there = jnp.max(jnp.where(here, 1.0, 0.0), axis=1, keepdims=True) > 0.5
        moved = mm(hot(here), down_ref[...])
        rows_copy(i).wait()
        pltpu.make_async_copy(lower_ref.at[rows_of(i)], lower_ref.at[rows_of(i)], lower_sem.at[i]).wait()
        old = rows_ref[rows_of(i), :]
        new = jnp.where(there, moved, old) - mm(lower_ref[rows_of(i), :], u_ref[...])
        in_top = i < NB // CHUNK
        top = u_ref[rows_of(i & (NB // CHUNK - 1)), :].astype(F32)
        new = jnp.where(in_top & (me == number), top, jnp.where(in_top & (me < number), old, new))
        rows_ref[rows_of(i), :] = new
        out_copy(i).start()
        return carry

    lax.fori_loop(0, count, step, 0, unroll=True)
    for i in range(count):
        out_copy(i).wait()


def update_kernel(number, matrix_ref, to_ref, m0, m1, m2, m3, *refs):
    lowers, out_ref, scratch = refs[: 2 - number], refs[2 - number], refs[3 - number :]
    update(number, matrix_ref, to_ref, (m0, m1, m2, m3), lowers, out_ref, scratch)


def ahead_kernel(from_ref, matrix_ref, top_ref, low_ref, rows_ref, panel_ref, held_ref, lower_ref, sems):
    count = 2 * NB // CHUNK
    pairs = []
    for i in range(count):
        chunk, inner = pl.ds(i * CHUNK, CHUNK), pl.ds(i * CHUNK % NB, CHUNK)
        pairs.append((matrix_ref.at[chunk], held_ref.at[chunk]))
        pairs.append(((top_ref, low_ref)[i * CHUNK // NB].at[inner], lower_ref.at[chunk]))
    moving = copies(pairs, sems)
    rows, panel = jnp.zeros((LANES, COLS), F32), jnp.zeros((LANES, NB), F32)
    for i in range(count):
        chunk = pl.ds(i * CHUNK, CHUNK)
        select = hot(from_ref[:, 2:3] == iota((LANES, CHUNK), 1) + i * CHUNK)
        moving[2 * i].wait()
        high, low = split(held_ref[chunk])
        rows = rows + (mm(select, high) + mm(select, low))
        moving[2 * i + 1].wait()
        panel = panel + mm(select, lower_ref[chunk])
    rows_ref[...] = rows
    panel_ref[...] = panel.astype(BF16)


def pivots_kernel(from_ref, to_ref, rows_ref, panel_ref, m0, m1, m2, m3, picked_ref, u_ref, down_ref):
    receive((m0, m1, m2, m3), u_ref, down_ref)
    same = jnp.where(from_ref[:, 2:3] == to_ref[1:2, :], 1.0, 0.0)
    moved = jnp.max(same, axis=1, keepdims=True) > 0.5
    rows = jnp.where(moved, mm(same.astype(BF16), down_ref[...]), rows_ref[...])
    high, low = split(rows - mm(panel_ref[...], u_ref[...]))
    picked_ref[:CAP] = high[:CAP]
    picked_ref[CAP:] = low[:CAP]


def send(value, pairs):
    return lax.ppermute(value, "row", pairs)


def over_x(root_x, pieces):
    return [pieces[root_x]] + [
        send(pieces[(root_x + s) % NX], [(at(0, root_x), at(0, root_x + s))]) for s in range(1, NX)
    ]


def in_hbm(a):
    return pltpu.with_memory_space_constraint(a, pltpu.HBM)


def from_front(messages):
    return [messages[0]] + [
        send(messages[z], [(at(0, x), at(z, x)) for x in range(NX)]) for z in range(1, NZ)
    ]


def along_x(messages):
    return [messages[0]] + [
        send(messages[s], [(at(z, x), at(z, x + s)) for z in range(NZ) for x in range(NX)])
        for s in range(1, NX)
    ]


def local(slab, lower_first, lower_second, pivot_rows, displaced):
    row = lax.axis_index("row")
    matrix = slab.reshape(2 * NB, COLS)
    first, second = [p.reshape(2 * NB, p.shape[3]) for p in (lower_first, lower_second)]
    gather = lambda block: lax.all_gather(block, "col", axis=1, tiled=True)
    picked_shape = ((2 * CAP, COLS), BF16)
    there, vmem = pl.BlockSpec(memory_space=pltpu.HBM), pl.BlockSpec(memory_space=pltpu.VMEM)
    block_of_top = pl.BlockSpec((NB, COLS), lambda i: (0, 0))
    update_scratch = [
        pltpu.VMEM((NB, COLS), BF16),
        pltpu.VMEM((LANES, COLS), BF16),
        pltpu.VMEM((2 * NB, COLS), F32),
        pltpu.VMEM((2 * NB, NB), BF16),
    ] + [pltpu.SemaphoreType.DMA((2 * NB // CHUNK,))] * 3
    inverse = lambda d: call(
        inverse_kernel,
        [((NB, HALF), BF16)] * 2 + [((HALF, HALF), BF16)],
        in_hbm(d),
        name="inverse",
        in_specs=[there],
        scratch=[pltpu.VMEM((NB, NB), BF16), pltpu.VMEM((NB // TILE, TILE, TILE), BF16)]
        + [pltpu.SemaphoreType.DMA((NB // TILE + 1,))],
        mib=24,
    )
    relayed = [((HALF + 2 * CAP, LANES), BF16)] * NX
    rows = jnp.stack([pivot_rows, displaced], axis=1).reshape(4, NB)
    top = gather(first[:NB])
    rows = jnp.concatenate([rows, rows], axis=0)
    slot, order, pivots, targets, picked = call(
        index_kernel,
        [((NB, LANES), I32), ((8, NB), I32), ((LANES, LANES), I32), ((8, LANES), I32), picked_shape],
        rows,
        in_hbm(matrix),
        name="index",
        in_specs=[vmem, there],
        scratch=[pltpu.VMEM((2 * NB, COLS), F32), pltpu.SemaphoreType.DMA((2 * NB // CHUNK,))],
    )
    late, picked = lax.optimization_barrier((first, picked))
    low = gather(late[NB:])

    by_x = [picked] + [
        send(picked, [(at(z, x + s), at(z, x)) for z in range(NZ) for x in range(NX)]) for s in range(1, NX)
    ]
    joined, own_down, *messages = call(
        first_front_kernel,
        [((FLOCK, 2 * COLS), BF16), ((FLOCK, COLS), BF16)] + [((FLOCK, 2 * COLS), BF16)] * (NZ - 1),
        matrix,
        order,
        *by_x,
        name="front",
        in_specs=[block_of_top] + [vmem] * 5,
        grid=(1,),
    )
    parts = [joined] + [
        in_hbm(send(message, [(at(z, 0), at(0, 0)), (at(0, 0), at(z, 0))]))
        for z, message in enumerate(messages, 1)
    ]
    inverses, parts[-1] = lax.optimization_barrier((inverse(top), parts[-1]))
    own_down, *solved = call(
        first_solve_kernel,
        [((FLOCK, COLS), BF16)] + [((HALF, LANES), BF16)] * NX,
        *inverses,
        slot,
        own_down,
        *parts,
        name="solve",
        in_specs=[vmem] * 6 + [there] * (NZ - 1),
        scratch=[pltpu.VMEM((NX * GROUP, 2 * COLS), BF16), pltpu.VMEM((3 * HALF, 2 * COLS), BF16)]
        + [pltpu.VMEM((NB, NX * GROUP), BF16)]
        + [pltpu.SemaphoreType.DMA((NZ,))],
        mib=20,
    )
    block, solved = lax.optimization_barrier((second[:NB], solved))
    hops = [send(block, [(at(0, 1), at(0, 2))])]
    pieces = over_x(0, solved)
    hops[0], pieces[-1] = lax.optimization_barrier((hops[0], pieces[-1]))
    hops.append(send(hops[0], [(at(0, 2), at(0, 3))]))
    piece = pieces[0]
    for s in range(1, NX):
        piece = jnp.where(row == s, pieces[s], piece)
    came = from_front([piece] * NZ)
    hops[1], came[1] = lax.optimization_barrier((hops[1], came[1]))
    hops.append(send(hops[1], [(at(0, 3), at(0, 0))]))
    messages = call(relay_kernel, relayed, piece, own_down, *came[1:], name="relay")
    hops, messages = lax.optimization_barrier((hops, messages))
    spread = along_x(messages)
    block = jnp.where(row == 1, block, hops[0] + hops[1] + hops[2])
    block, late = lax.optimization_barrier((block, second))
    diag, lower = gather(block), gather(late)
    top, low = in_hbm(top), in_hbm(low)
    ready, late = lax.optimization_barrier((pivots, spread[0]))
    ahead = call(
        ahead_kernel,
        [((LANES, COLS), F32), ((LANES, NB), BF16)],
        ready,
        in_hbm(matrix),
        top,
        low,
        name="ahead",
        in_specs=[vmem] + [there] * 3,
        scratch=update_scratch[2:4] + [pltpu.SemaphoreType.DMA((4 * NB // CHUNK,))],
        mib=16,
    )
    (picked,) = call(
        pivots_kernel,
        [picked_shape],
        pivots,
        targets,
        *ahead,
        *spread,
        name="pivots",
        scratch=update_scratch[:2],
    )
    came = [picked] + [send(picked, [(at(z, x), at(0, x)) for x in range(NX)]) for z in range(1, NZ)]
    (matrix,) = call(
        functools.partial(update_kernel, 0),
        [((2 * NB, COLS), F32)],
        matrix,
        targets,
        *spread,
        top,
        low,
        name="update",
        scratch=update_scratch,
        mib=16,
        in_specs=[there] + [vmem] * 5 + [there] * 2,
        out_specs=[there],
    )
    matrix, came[-1] = lax.optimization_barrier((matrix, came[-1]))
    order, came[3] = lax.optimization_barrier((order, came[3]))
    (downs,) = call(
        last_down_kernel,
        [((2 * NZ * FLOCK, LANES), BF16)],
        matrix,
        order,
        name="down",
        in_specs=[block_of_top, vmem],
        grid=(1,),
    )
    cuts = call(cut_kernel, [((GROUP, LANES), BF16)] * NX, *came, name="cut")
    cuts = along_x(cuts)
    cuts = cuts[:1] + [in_hbm(cut) for cut in cuts[1:]]
    messages = call(
        last_solve_kernel,
        [((HALF + 2 * FLOCK, LANES), BF16)] * NZ,
        *inverse(diag),
        slot,
        downs,
        *cuts,
        name="solve",
        in_specs=[vmem] * 6 + [there] * (NX - 1),
        scratch=[pltpu.VMEM((NX * GROUP, LANES), BF16), pltpu.VMEM((NB, NX * GROUP), BF16)]
        + [pltpu.SemaphoreType.DMA((NX,))],
        mib=20,
    )
    relay_scratch = [pltpu.VMEM((FLOCK, COLS), BF16)]
    messages = call(last_relay_kernel, relayed, *from_front(messages), name="relay", scratch=relay_scratch)
    (matrix,) = call(
        functools.partial(update_kernel, 1),
        [((2 * NB, COLS), F32)],
        matrix,
        targets,
        *along_x(messages),
        in_hbm(lower),
        name="update",
        scratch=update_scratch,
        mib=16,
        in_specs=[there] + [vmem] * 5 + [there],
        out_specs=[there],
    )
    return matrix.reshape(2, 1, NB, COLS)


def solution(mesh):
    placed = (
        P(None, "row", None, "col"),
        P(None, "row", None, "col"),
        P(None, "row", None, "col"),
        P(),
        P(),
    )
    return jax.shard_map(
        local, mesh=mesh, in_specs=placed, out_specs=P(None, "row", None, "col"), check_vma=False
    )
```

```python
import functools

import jax
import jax.numpy as jnp
from jax import lax
from jax.experimental import pallas as pl
from jax.experimental.pallas import tpu as pltpu
from jax.sharding import PartitionSpec as P

NB = 1024
CAP = 48
NX, NZ, NY = 4, 8, 4
TILE = 128
LANES = 128
CHUNK = 512
FLOCK = NX * CAP
HALF = NB // 2
GROUP = NZ * CAP
COLS = 256
PART = COLS // NX
BF16, F32, I32 = jnp.bfloat16, jnp.float32, jnp.int32


def at(z, x):
    return (z % NZ) * NX + x % NX


def mm(a, b):
    return jnp.dot(a, b, preferred_element_type=F32)


def mm_t(a, b):
    return lax.dot_general(a, b, (((0,), (0,)), ((), ())), preferred_element_type=F32)


def iota(shape, axis):
    return lax.broadcasted_iota(I32, shape, axis)


def hot(mask):
    return jnp.where(mask, 1.0, 0.0).astype(BF16)


def split(value):
    high = value.astype(BF16)
    return high, (value - high.astype(F32)).astype(BF16)


def call(kernel, outs, *args, name, scratch=(), mib=10, **blocks):
    size = lambda a: a.size * a.dtype.itemsize
    return pl.pallas_call(
        kernel,
        out_shape=[jax.ShapeDtypeStruct(s, d) for s, d in outs],
        scratch_shapes=list(scratch),
        compiler_params=pltpu.CompilerParams(vmem_limit_bytes=mib * 2**20),
        cost_estimate=pl.CostEstimate(
            flops=0, bytes_accessed=sum(size(a) for a in args), transcendentals=0
        ),
        name=name,
        **blocks,
    )(*args)


def copies(pairs, sems):
    made = [pltpu.make_async_copy(source, target, sems.at[i]) for i, (source, target) in enumerate(pairs)]
    for copy in made:
        copy.start()
    return made


def place_in(rows):
    return ((rows >> 15) << 10) | (rows & (NB - 1))


def owner_of(rows):
    return (rows >> 10) & 31


def x_major(owner, rank):
    return ((owner & (NX - 1)) * NZ + (owner >> 2)) * CAP + rank


def index_kernel(rows_ref, matrix_ref, slot_ref, order_ref, from_ref, to_ref, picked_ref, held_ref, sems):
    chunks = [pl.ds(i * CHUNK, CHUNK) for i in range(2 * NB // CHUNK)]
    moving = copies([(matrix_ref.at[chunk], held_ref.at[chunk]) for chunk in chunks], sems)
    me = lax.axis_index("row")
    cols = rows_ref[...].astype(F32).T.astype(I32)
    lane = iota((NB, LANES), 1)
    owners = jnp.zeros((NB, LANES), I32)
    for k in range(4):
        owners = jnp.where(lane >> 5 == k, owner_of(cols[:, k : k + 1]), owners)
    own = jnp.where(owners == (lane & 31), 1.0, 0.0)
    earlier = hot(iota((TILE, TILE), 1) < iota((TILE, TILE), 0))
    before, count = [], jnp.zeros((1, LANES), F32)
    for i in range(NB // TILE):
        part = own[i * TILE : (i + 1) * TILE]
        before.append((mm(earlier, part.astype(BF16)) + count) * part)
        count = count + jnp.sum(part, axis=0, keepdims=True)
    before = jnp.concatenate(before, axis=0)
    slots, lists = jnp.zeros((NB, LANES), I32), jnp.zeros((LANES, LANES), I32)
    row, line = iota((8, NB), 0), iota((LANES, LANES), 0)
    for k in range(4):
        owner = owner_of(cols[:, k : k + 1])
        rank = jnp.sum(jnp.where(lane >> 5 == k, before, 0.0), axis=1, keepdims=True).astype(I32)
        slots = jnp.where(lane == k, x_major(owner, rank), slots)
        mine = hot((owner == me) & (rank == lane) & (lane < CAP))
        place = place_in(rows_ref[k : k + 1, :])
        parts = jnp.where(row == 0, place >> 6, jnp.where(row == 1, place & 63, 1))
        found = mm(parts.astype(F32).astype(BF16), mine).astype(I32)
        places = jnp.where(found[2:3] > 0, found[:1] * 64 + found[1:2], -1)
        lists = jnp.where(line == k, places, lists)
    slot_ref[...] = slots
    order_ref[...] = slots.astype(F32).T[:8].astype(I32)
    to_ref[...] = lists[:8]
    from_ref[...] = lists.astype(F32).T.astype(I32)
    high = low = jnp.zeros((LANES, COLS), F32)
    for i, chunk in enumerate(chunks):
        moving[i].wait()
        some = pick(0, from_ref, i * CHUNK, held_ref[chunk])
        high, low = high + some[0], low + some[1]
    picked_ref[:CAP] = high[:CAP].astype(BF16)
    picked_ref[CAP:] = low[:CAP].astype(BF16)


def pick(number, from_ref, start, rows):
    select = hot(from_ref[:, 2 * number : 2 * number + 1] == iota((LANES, rows.shape[0]), 1) + start)
    high, low = split(rows)
    return mm(select, high), mm(select, low)


def down(number, z, top, order_ref):
    line = iota((FLOCK, 1), 0)
    slot = line + z * CAP
    for k in range(1, NX):
        slot = slot + jnp.where(line >= k * CAP, GROUP - CAP, 0)
    order = order_ref[2 * number + 1 : 2 * number + 2, :]
    return mm(hot(order == slot), top).astype(BF16)


def first_front_kernel(top_ref, order_ref, b0, b1, b2, b3, joined_ref, own_ref, *outs):
    for s, ref in enumerate((b0, b1, b2, b3)):
        joined_ref[s * CAP : (s + 1) * CAP, :COLS] = ref[:CAP]
        joined_ref[s * CAP : (s + 1) * CAP, COLS:] = ref[CAP:]
    own_ref[...] = jnp.zeros_like(own_ref)
    is_root = lax.axis_index("row") == 0

    @pl.when(is_root)
    def _():
        top = top_ref[...].astype(BF16)
        own_ref[...] = down(0, 0, top, order_ref)
        for z, ref in enumerate(outs):
            ref[:, :COLS] = down(0, z + 1, top, order_ref)
            ref[:, COLS:] = jnp.zeros((FLOCK, COLS), BF16)

    @pl.when(jnp.logical_not(is_root))
    def _():
        for ref in outs:
            ref[...] = joined_ref[...]


def last_down_kernel(top_ref, order_ref, out_ref):
    out_ref[...] = jnp.zeros_like(out_ref)

    @pl.when(lax.axis_index("row") == 1)
    def _():
        top = top_ref[...].astype(BF16)
        for z in range(NZ):
            rows = down(1, z, top, order_ref)
            out_ref[2 * z * FLOCK : (2 * z + 1) * FLOCK] = rows[:, :LANES]
            out_ref[(2 * z + 1) * FLOCK : (2 * z + 2) * FLOCK] = rows[:, LANES:]


def cut_kernel(*refs):
    picked, outs = refs[:NZ], refs[NZ:]
    x = lax.axis_index("row") & (NX - 1)
    high = jnp.concatenate([p[:CAP] for p in picked], axis=0)
    low = jnp.concatenate([p[CAP:] for p in picked], axis=0)
    row, lane = iota((COLS, LANES), 0), iota((COLS, LANES), 1)
    for s, ref in enumerate(outs):
        first = ((x + s) & (NX - 1)) * PART
        left = hot((row == first + lane) & (lane < PART))
        right = hot((row == first + lane - PART) & (lane >= PART))
        ref[...] = (mm(high, left) + mm(low, right)).astype(BF16)


def mm3(a, b):
    a_high, a_low = split(a)
    b_high, b_low = split(b)
    return mm(a_high, b_high) + (mm(a_high, b_low) + mm(a_low, b_high))


def inverse_kernel(diag_hbm, high_ref, low_ref, below_ref, diag_ref, tile_ref, sems):
    count = NB // TILE
    parts = [pl.ds(i * TILE, TILE) for i in range(count)]
    pairs = [(diag_hbm.at[part, part], tile_ref.at[i]) for i, part in enumerate(parts)]
    moving = copies(pairs + [(diag_hbm, diag_ref)], sems)
    row, lane = iota((TILE, TILE), 0), iota((TILE, TILE), 1)
    identity = jnp.where(lane == row, 1.0, 0.0)
    powers = []
    for i in range(count):
        moving[i].wait()
        powers.append(jnp.where(lane < row, -tile_ref[i].astype(F32), 0.0))
    inverses = [identity + p for p in powers]
    for _ in range(TILE.bit_length() - 2):
        powers = [mm3(p, p) for p in powers]
        inverses = [v + mm3(v, p) for v, p in zip(inverses, powers)]
    size = TILE
    moving[count].wait()
    below_ref[...] = diag_ref[HALF:, :HALF]
    while size < HALF:
        none = jnp.zeros((size, size), F32)
        joined = []
        for i in range(0, len(inverses), 2):
            upper, lower = inverses[i], inverses[i + 1]
            between = diag_ref[(i + 1) * size : (i + 2) * size, i * size : (i + 1) * size]
            high, low = split(upper)
            corner = mm3(lower, mm(between, high) + mm(between, low))
            joined.append(
                jnp.concatenate(
                    [
                        jnp.concatenate([upper, none], axis=1),
                        jnp.concatenate([-corner, lower], axis=1),
                    ],
                    axis=0,
                )
            )
        inverses, size = joined, 2 * size
    for i, value in enumerate(inverses):
        part = slice(i * HALF, (i + 1) * HALF)
        high_ref[part], low_ref[part] = split(value)


def first_solve_kernel(high_ref, low_ref, below_ref, slot_ref, own_ref, *refs):
    parts, down_ref, outs = refs[:NZ], refs[NZ], refs[NZ + 1 : NZ + 1 + NX]
    gathered_ref, right_ref, select_ref, sems = refs[NZ + 1 + NX :]
    places = [slice(z * FLOCK, (z + 1) * FLOCK) for z in range(NZ)]
    pairs = [(part, gathered_ref.at[place]) for part, place in zip(parts[1:], places[1:])]
    moving = copies(pairs, sems)
    gathered_ref[places[0]] = parts[0][...]
    lane = iota((1, FLOCK), 1)
    for k in range(1, NX):
        lane = lane + jnp.where(iota((1, FLOCK), 1) >= k * CAP, GROUP - CAP, 0)
    for z, place in enumerate(places):
        select_ref[:, place] = hot(slot_ref[:, :1] == lane + z * CAP)
    for copy in moving:
        copy.wait()
    came = gathered_ref[places[1], :COLS]
    for place in places[2:]:
        came = came + gathered_ref[place, :COLS]
    down_ref[...] = jnp.where(lax.axis_index("row") == 0, own_ref[...], came)

    def wide_parts(place, value):
        part = slice(place * HALF, (place + 1) * HALF)
        right_ref[part, :COLS], right_ref[part, COLS:] = split(value)
        return right_ref[part]

    def fold(wide):
        return wide[:, :COLS] + wide[:, COLS:]

    found = [fold(mm(select_ref[i : i + HALF], gathered_ref[...])) for i in range(0, NB, HALF)]
    first = wide_parts(0, found[0])
    upper = fold(mm(high_ref[:HALF], first)) + mm(low_ref[:HALF], first[:, :COLS])
    second = wide_parts(2, found[1] - fold(mm(below_ref[...], wide_parts(1, upper))))
    lower = fold(mm(high_ref[HALF:], second)) + mm(low_ref[HALF:], second[:, :COLS])
    halves = [upper, lower]
    left = iota((HALF, LANES), 1) < PART
    for x, ref in enumerate(outs):
        block = slice(x // 2 * LANES, (x // 2 + 1) * LANES)
        upper, lower = halves[0][:, block], halves[1][:, block]
        if x % 2 == 0:
            ref[...] = jnp.where(left, upper, pltpu.roll(lower, PART, 1)).astype(BF16)
        else:
            ref[...] = jnp.where(left, pltpu.roll(upper, PART, 1), lower).astype(BF16)


def both(value):
    return value + pltpu.roll(value, PART, 1)


def last_solve_kernel(high_ref, low_ref, below_ref, slot_ref, down_ref, c0, c1, c2, c3, *refs):
    outs, (gathered_ref, select_ref, sems) = refs[:NZ], refs[NZ:]
    x = lax.axis_index("row") & (NX - 1)
    parts = [slice(s * GROUP, (s + 1) * GROUP) for s in range(NX)]
    pairs = [(ref, gathered_ref.at[part]) for ref, part in zip((c1, c2, c3), parts[1:])]
    moving = copies(pairs, sems)
    gathered_ref[parts[0]] = c0[...]
    for s, part in enumerate(parts):
        first = ((x - s) & (NX - 1)) * GROUP
        select_ref[:, part] = hot(slot_ref[:, 2:3] == iota((1, GROUP), 1) + first)
    for copy in moving:
        copy.wait()
    left = iota((HALF, LANES), 1) < PART
    halves = []
    for i in range(0, NB, HALF):
        found = both(mm(select_ref[i : i + HALF], gathered_ref[...]))
        if i > 0:
            high, low = split(halves[0])
            found = found - both(mm(below_ref[...], jnp.where(left, high, low)))
        high, low = split(found)
        wide = both(mm(high_ref[i : i + HALF], jnp.where(left, high, low)))
        halves.append(wide + mm(low_ref[i : i + HALF], high))
    solved = jnp.where(left, halves[0], halves[1]).astype(BF16)
    for z, ref in enumerate(outs):
        ref[:HALF] = solved
        ref[HALF:] = down_ref[2 * z * FLOCK : 2 * (z + 1) * FLOCK]


def pass_on(solved, rows_ref, outs):
    x = lax.axis_index("row") & (NX - 1)
    for s, ref in enumerate(outs):
        start = pl.multiple_of(((x + s) & (NX - 1)) * CAP, CAP)
        rows = rows_ref[pl.ds(start, CAP), :]
        ref[:HALF] = solved
        ref[HALF : HALF + CAP] = rows[:, :LANES]
        ref[HALF + CAP :] = rows[:, LANES:]


def sum_of(refs, part):
    total = refs[0][part]
    for ref in refs[1:]:
        total = total + ref[part]
    return total


def relay_kernel(own_ref, down_ref, *refs):
    came, outs = refs[: NZ - 1], refs[NZ - 1 :]
    front = lax.axis_index("row") < NX
    pass_on(jnp.where(front, own_ref[...], sum_of(came, slice(None))), down_ref, outs)


def last_relay_kernel(own_ref, *refs):
    came, outs, rows_ref = refs[: NZ - 1], refs[NZ - 1 : -1], refs[-1]
    front = lax.axis_index("row") < NX
    message = jnp.where(front, own_ref[...], sum_of(came, slice(None)))
    rows_ref[:, :LANES] = message[HALF : HALF + FLOCK]
    rows_ref[:, LANES:] = message[HALF + FLOCK :]
    pass_on(message[:HALF], rows_ref, outs)


def receive(pieces, u_ref, down_ref):
    x = lax.axis_index("row") & (NX - 1)
    row, lane = iota((LANES, COLS), 0), iota((LANES, COLS), 1)
    above, below = jnp.zeros((HALF, COLS), F32), jnp.zeros((HALF, COLS), F32)
    for s, ref in enumerate(pieces):
        first = ((x - s) & (NX - 1)) * PART
        piece = ref[:HALF]
        above = above + mm(piece, hot((lane == first + row) & (row < PART)))
        below = below + mm(piece, hot((lane == first + row - PART) & (row >= PART)))
    u_ref[:HALF] = above.astype(BF16)
    u_ref[HALF:] = below.astype(BF16)
    down_ref[:CAP, :LANES] = sum_of(pieces, slice(HALF, HALF + CAP))
    down_ref[:CAP, LANES:] = sum_of(pieces, slice(HALF + CAP, HALF + 2 * CAP))
    down_ref[CAP:] = jnp.zeros((LANES - CAP, COLS), BF16)


def update(number, matrix_ref, to_ref, pieces, lower_refs, out_ref, scratch):
    u_ref, down_ref, rows_ref, lower_ref, rows_sem, lower_sem, out_sem = scratch
    me = lax.axis_index("row")
    count = 2 * NB // CHUNK
    each = count // len(lower_refs)

    def rows_of(i):
        return pl.ds(pl.multiple_of(i * CHUNK, CHUNK), CHUNK)

    def rows_copy(i):
        return pltpu.make_async_copy(matrix_ref.at[rows_of(i)], rows_ref.at[rows_of(i)], rows_sem.at[i])

    def out_copy(i):
        return pltpu.make_async_copy(rows_ref.at[rows_of(i)], out_ref.at[rows_of(i)], out_sem.at[i])

    for i in range(count):
        rows_copy(i).start()
        source = lower_refs[i // each].at[rows_of(i % each)]
        pltpu.make_async_copy(source, lower_ref.at[rows_of(i)], lower_sem.at[i]).start()
    receive(pieces, u_ref, down_ref)

    def step(i, carry):
        here = to_ref[2 * number + 1 : 2 * number + 2, :] == iota((CHUNK, LANES), 0) + i * CHUNK
        there = jnp.max(jnp.where(here, 1.0, 0.0), axis=1, keepdims=True) > 0.5
        moved = mm(hot(here), down_ref[...])
        rows_copy(i).wait()
        pltpu.make_async_copy(lower_ref.at[rows_of(i)], lower_ref.at[rows_of(i)], lower_sem.at[i]).wait()
        old = rows_ref[rows_of(i), :]
        new = jnp.where(there, moved, old) - mm(lower_ref[rows_of(i), :], u_ref[...])
        in_top = i < NB // CHUNK
        top = u_ref[rows_of(i & (NB // CHUNK - 1)), :].astype(F32)
        new = jnp.where(in_top & (me == number), top, jnp.where(in_top & (me < number), old, new))
        rows_ref[rows_of(i), :] = new
        out_copy(i).start()
        return carry

    lax.fori_loop(0, count, step, 0, unroll=True)
    for i in range(count):
        out_copy(i).wait()


def update_kernel(number, matrix_ref, to_ref, m0, m1, m2, m3, *refs):
    lowers, out_ref, scratch = refs[: 2 - number], refs[2 - number], refs[3 - number :]
    update(number, matrix_ref, to_ref, (m0, m1, m2, m3), lowers, out_ref, scratch)


def ahead_kernel(from_ref, matrix_ref, top_ref, low_ref, rows_ref, panel_ref, held_ref, lower_ref, sems):
    count = 2 * NB // CHUNK
    pairs = []
    for i in range(count):
        chunk, inner = pl.ds(i * CHUNK, CHUNK), pl.ds(i * CHUNK % NB, CHUNK)
        pairs.append((matrix_ref.at[chunk], held_ref.at[chunk]))
        pairs.append(((top_ref, low_ref)[i * CHUNK // NB].at[inner], lower_ref.at[chunk]))
    moving = copies(pairs, sems)
    rows, panel = jnp.zeros((LANES, COLS), F32), jnp.zeros((LANES, NB), F32)
    for i in range(count):
        chunk = pl.ds(i * CHUNK, CHUNK)
        select = hot(from_ref[:, 2:3] == iota((LANES, CHUNK), 1) + i * CHUNK)
        moving[2 * i].wait()
        high, low = split(held_ref[chunk])
        rows = rows + (mm(select, high) + mm(select, low))
        moving[2 * i + 1].wait()
        panel = panel + mm(select, lower_ref[chunk])
    rows_ref[...] = rows
    panel_ref[...] = panel.astype(BF16)


def pivots_kernel(from_ref, to_ref, rows_ref, panel_ref, m0, m1, m2, m3, picked_ref, u_ref, down_ref):
    receive((m0, m1, m2, m3), u_ref, down_ref)
    same = jnp.where(from_ref[:, 2:3] == to_ref[1:2, :], 1.0, 0.0)
    moved = jnp.max(same, axis=1, keepdims=True) > 0.5
    rows = jnp.where(moved, mm(same.astype(BF16), down_ref[...]), rows_ref[...])
    high, low = split(rows - mm(panel_ref[...], u_ref[...]))
    picked_ref[:CAP] = high[:CAP]
    picked_ref[CAP:] = low[:CAP]


def send(value, pairs):
    return lax.ppermute(value, "row", pairs)


def over_x(root_x, pieces):
    return [pieces[root_x]] + [
        send(pieces[(root_x + s) % NX], [(at(0, root_x), at(0, root_x + s))]) for s in range(1, NX)
    ]


def in_hbm(a):
    return pltpu.with_memory_space_constraint(a, pltpu.HBM)


def from_front(messages):
    return [messages[0]] + [
        send(messages[z], [(at(0, x), at(z, x)) for x in range(NX)]) for z in range(1, NZ)
    ]


def along_x(messages):
    return [messages[0]] + [
        send(messages[s], [(at(z, x), at(z, x + s)) for z in range(NZ) for x in range(NX)])
        for s in range(1, NX)
    ]


def local(slab, lower_first, lower_second, pivot_rows, displaced):
    row = lax.axis_index("row")
    matrix = slab.reshape(2 * NB, COLS)
    first, second = [p.reshape(2 * NB, p.shape[3]) for p in (lower_first, lower_second)]
    gather = lambda block: lax.all_gather(block, "col", axis=1, tiled=True)
    picked_shape = ((2 * CAP, COLS), BF16)
    there, vmem = pl.BlockSpec(memory_space=pltpu.HBM), pl.BlockSpec(memory_space=pltpu.VMEM)
    block_of_top = pl.BlockSpec((NB, COLS), lambda i: (0, 0))
    update_scratch = [
        pltpu.VMEM((NB, COLS), BF16),
        pltpu.VMEM((LANES, COLS), BF16),
        pltpu.VMEM((2 * NB, COLS), F32),
        pltpu.VMEM((2 * NB, NB), BF16),
    ] + [pltpu.SemaphoreType.DMA((2 * NB // CHUNK,))] * 3
    inverse = lambda d: call(
        inverse_kernel,
        [((NB, HALF), BF16)] * 2 + [((HALF, HALF), BF16)],
        in_hbm(d),
        name="inverse",
        in_specs=[there],
        scratch=[pltpu.VMEM((NB, NB), BF16), pltpu.VMEM((NB // TILE, TILE, TILE), BF16)]
        + [pltpu.SemaphoreType.DMA((NB // TILE + 1,))],
        mib=24,
    )
    relayed = [((HALF + 2 * CAP, LANES), BF16)] * NX
    rows = jnp.stack([pivot_rows, displaced], axis=1).reshape(4, NB)
    top = gather(first[:NB])
    rows = jnp.concatenate([rows, rows], axis=0)
    slot, order, pivots, targets, picked = call(
        index_kernel,
        [((NB, LANES), I32), ((8, NB), I32), ((LANES, LANES), I32), ((8, LANES), I32), picked_shape],
        rows,
        in_hbm(matrix),
        name="index",
        in_specs=[vmem, there],
        scratch=[pltpu.VMEM((2 * NB, COLS), F32), pltpu.SemaphoreType.DMA((2 * NB // CHUNK,))],
    )
    late, picked = lax.optimization_barrier((first, picked))
    low = gather(late[NB:])

    by_x = [picked] + [
        send(picked, [(at(z, x + s), at(z, x)) for z in range(NZ) for x in range(NX)]) for s in range(1, NX)
    ]
    joined, own_down, *messages = call(
        first_front_kernel,
        [((FLOCK, 2 * COLS), BF16), ((FLOCK, COLS), BF16)] + [((FLOCK, 2 * COLS), BF16)] * (NZ - 1),
        matrix,
        order,
        *by_x,
        name="front",
        in_specs=[block_of_top] + [vmem] * 5,
        grid=(1,),
    )
    parts = [joined] + [
        in_hbm(send(message, [(at(z, 0), at(0, 0)), (at(0, 0), at(z, 0))]))
        for z, message in enumerate(messages, 1)
    ]
    inverses, parts[-1] = lax.optimization_barrier((inverse(top), parts[-1]))
    own_down, *solved = call(
        first_solve_kernel,
        [((FLOCK, COLS), BF16)] + [((HALF, LANES), BF16)] * NX,
        *inverses,
        slot,
        own_down,
        *parts,
        name="solve",
        in_specs=[vmem] * 6 + [there] * (NZ - 1),
        scratch=[pltpu.VMEM((NX * GROUP, 2 * COLS), BF16), pltpu.VMEM((3 * HALF, 2 * COLS), BF16)]
        + [pltpu.VMEM((NB, NX * GROUP), BF16)]
        + [pltpu.SemaphoreType.DMA((NZ,))],
        mib=20,
    )
    block, solved = lax.optimization_barrier((second[:NB], solved))
    hops = [send(block, [(at(0, 1), at(0, x))]) for x in (2, 0)]
    pieces = over_x(0, solved)
    hops[0], pieces[-1] = lax.optimization_barrier((hops[0], pieces[-1]))
    hops.append(send(hops[0], [(at(0, 2), at(0, 3))]))
    piece = pieces[0]
    for s in range(1, NX):
        piece = jnp.where(row == s, pieces[s], piece)
    came = from_front([piece] * NZ)
    messages = call(relay_kernel, relayed, piece, own_down, *came[1:], name="relay")
    hops, messages = lax.optimization_barrier((hops, messages))
    spread = along_x(messages)
    block = jnp.where(row == 1, block, hops[0] + hops[1] + hops[2])
    block, late = lax.optimization_barrier((block, second))
    diag, lower = gather(block), gather(late)
    top, low = in_hbm(top), in_hbm(low)
    ready, late = lax.optimization_barrier((pivots, spread[0]))
    ahead = call(
        ahead_kernel,
        [((LANES, COLS), F32), ((LANES, NB), BF16)],
        ready,
        in_hbm(matrix),
        top,
        low,
        name="ahead",
        in_specs=[vmem] + [there] * 3,
        scratch=update_scratch[2:4] + [pltpu.SemaphoreType.DMA((4 * NB // CHUNK,))],
        mib=16,
    )
    (picked,) = call(
        pivots_kernel,
        [picked_shape],
        pivots,
        targets,
        *ahead,
        *spread,
        name="pivots",
        scratch=update_scratch[:2],
    )
    came = [picked] + [send(picked, [(at(z, x), at(0, x)) for x in range(NX)]) for z in range(1, NZ)]
    (matrix,) = call(
        functools.partial(update_kernel, 0),
        [((2 * NB, COLS), F32)],
        matrix,
        targets,
        *spread,
        top,
        low,
        name="update",
        scratch=update_scratch,
        mib=16,
        in_specs=[there] + [vmem] * 5 + [there] * 2,
        out_specs=[there],
    )
    matrix, came[-1] = lax.optimization_barrier((matrix, came[-1]))
    order, came[3] = lax.optimization_barrier((order, came[3]))
    (downs,) = call(
        last_down_kernel,
        [((2 * NZ * FLOCK, LANES), BF16)],
        matrix,
        order,
        name="down",
        in_specs=[block_of_top, vmem],
        grid=(1,),
    )
    cuts = call(cut_kernel, [((GROUP, LANES), BF16)] * NX, *came, name="cut")
    cuts = along_x(cuts)
    cuts = cuts[:1] + [in_hbm(cut) for cut in cuts[1:]]
    messages = call(
        last_solve_kernel,
        [((HALF + 2 * FLOCK, LANES), BF16)] * NZ,
        *inverse(diag),
        slot,
        downs,
        *cuts,
        name="solve",
        in_specs=[vmem] * 6 + [there] * (NX - 1),
        scratch=[pltpu.VMEM((NX * GROUP, LANES), BF16), pltpu.VMEM((NB, NX * GROUP), BF16)]
        + [pltpu.SemaphoreType.DMA((NX,))],
        mib=20,
    )
    relay_scratch = [pltpu.VMEM((FLOCK, COLS), BF16)]
    messages = call(last_relay_kernel, relayed, *from_front(messages), name="relay", scratch=relay_scratch)
    (matrix,) = call(
        functools.partial(update_kernel, 1),
        [((2 * NB, COLS), F32)],
        matrix,
        targets,
        *along_x(messages),
        in_hbm(lower),
        name="update",
        scratch=update_scratch,
        mib=16,
        in_specs=[there] + [vmem] * 5 + [there],
        out_specs=[there],
    )
    return matrix.reshape(2, 1, NB, COLS)


def solution(mesh):
    placed = (
        P(None, "row", None, "col"),
        P(None, "row", None, "col"),
        P(None, "row", None, "col"),
        P(),
        P(),
    )
    return jax.shard_map(
        local, mesh=mesh, in_specs=placed, out_specs=P(None, "row", None, "col"), check_vma=False
    )
```
